512 devices in a mesh: ctx: 64 (over x, z, y_hi), head: 8 (over y_lo, core).
Axes of the slice: x: 4, y: 8 (y_hi: 2, y_lo: 4; y = y_hi * 4 + y_lo), z: 8, core: 2. Of those that a mesh axis runs over, the one named last changes fastest.
Arguments:
- pairing: int32 [64], replicated, may hold values from 0 to 63, as said below
- doc_start: int32 [16384], P('ctx'), may hold values from 0 to 16383, as said below
- block_live: int32 [128, 128], replicated, may hold values from 0 to 1, as said below
- query: bfloat16 [16384, 4096], P(('ctx', 'head')), may hold values from -24 to 24
- key: bfloat16 [16384, 1024], P(('ctx', 'head')), may hold values from -24 to 24
- value: bfloat16 [16384, 1024], P(('ctx', 'head')), may hold values from -6 to 6
- grad_out: bfloat16 [16384, 4096], P(('ctx', 'head')), may hold values from -6 to 6
Outputs:
- attended: bfloat16 [16384, 4096], P(('ctx', 'head'))
- grad_query: bfloat16 [16384, 4096], P(('ctx', 'head'))
- grad_key: bfloat16 [16384, 1024], P(('ctx', 'head'))
- grad_value: bfloat16 [16384, 1024], P(('ctx', 'head'))
The draws below stay inside these ranges and needn't reach their ends.
Inputs may be any that keep to these rules, and one draw needn't show every extreme that they name: pairing[pairing[c]] == c, and pairing[c] differs from c by at most 1. doc_start of a row is the position of the first token of its document; documents are runs of consecutive positions, the first starts at 0, each has 64 to 512 tokens except the last, which may be shorter, and one has exactly 512. block_live[a, b] == 1 exactly when b < a and the first token of global block a has doc_start at or before the last position of global block b.
All inputs are finite; a program needn't handle non-finite values.
Results may differ from the reference program's by a relative error of at most 0.03.
Values may be sent and summed in bfloat16 or wider, within the bound.
No kernel may reach another device: no remote copies, remote signals or barrier semaphores. Data moves between devices by JAX's collectives and lax.ppermute only.
A program may use at most 64 MiB of HBM per device.

```python
import jax
import jax.numpy as jnp
from jax import lax

HEADS = 32
KV_HEADS = 8
HEAD_DIM = 128
BLOCK = 128
REACH = 4
DOC_MOST = 512
SHORTEST = 64
BLOCKS = 128
TOKENS = 16384


def layout_blocks(partner):
    pair_count = partner.shape[0]
    device_ids = jnp.arange(pair_count, dtype=jnp.int32)
    return jnp.stack([device_ids, 2 * pair_count - 1 - partner], axis=1).reshape(-1)


def structure(key):
    pair_count = BLOCKS // 2
    phase_shift = jax.random.randint(jax.random.fold_in(key, 201), (), 0, 2)
    swap_bits = jax.random.randint(jax.random.fold_in(key, 202), (pair_count,), 0, 2)
    device = jnp.arange(pair_count, dtype=jnp.int32)
    couple = jnp.floor_divide(device - phase_shift, 2)
    lower_member = 2 * couple + phase_shift
    paired = (lower_member >= 0) & (lower_member + 1 < pair_count) & (swap_bits[jnp.clip(couple, 0, pair_count - 1)] == 1)
    partner = jnp.where(paired, jnp.where(device == lower_member, device + 1, device - 1), device).astype(jnp.int32)
    documents = TOKENS // SHORTEST + 1
    spread = jax.random.randint(jax.random.fold_in(key, 203), (documents,), 0, DOC_MOST - SHORTEST + 1)
    doc_kind = jax.random.randint(jax.random.fold_in(key, 204), (documents,), 0, 3)
    lengths = jnp.where(doc_kind == 0, DOC_MOST - spread // 8, SHORTEST + spread // 2)
    lengths = lengths.at[2].set(DOC_MOST).astype(jnp.int32)
    starts = jnp.cumsum(lengths) - lengths
    start_marks = jnp.zeros((TOKENS,), jnp.int32).at[starts].set(1, mode='drop')
    places = jnp.arange(TOKENS, dtype=jnp.int32)
    begins = lax.cummax(places * start_marks, axis=0)
    first_begin = begins.reshape(BLOCKS, BLOCK)[:, 0]
    block_ids = jnp.arange(BLOCKS, dtype=jnp.int32)
    last_place = (block_ids + 1) * BLOCK - 1
    reachable = (block_ids[None, :] < block_ids[:, None]) & (first_begin[:, None] <= last_place[None, :])
    ordered = begins.reshape(BLOCKS, BLOCK)[layout_blocks(partner)].reshape(-1)
    return (partner, ordered, reachable.astype(jnp.int32))


def draw_pairing(key, part):
    partner, ordered, reachable = structure(key)
    return partner


def draw_doc_start(key, part):
    partner, ordered, reachable = structure(key)
    return ordered


def draw_block_live(key, part):
    partner, ordered, reachable = structure(key)
    return reachable


def draw_query(key, part):
    key = jax.random.fold_in(key, 11)
    values = jnp.clip(jax.random.normal(key, (TOKENS, HEADS, HEAD_DIM)), -6.0, 6.0)
    return values.reshape(TOKENS, HEADS * HEAD_DIM).astype(jnp.bfloat16)


def draw_key(key, part):
    key = jax.random.fold_in(key, 12)
    values = jnp.clip(jax.random.normal(key, (TOKENS, KV_HEADS, HEAD_DIM)), -6.0, 6.0)
    return values.reshape(TOKENS, KV_HEADS * HEAD_DIM).astype(jnp.bfloat16)


def levels(rng, dims, shards, least, top_value):
    level, own = 1.0, jax.random.fold_in(rng, 6)
    for dim, shards_of in shards:
        heights = jnp.exp(jax.random.uniform(jax.random.fold_in(own, dim), (shards_of,), jnp.float32, least / len(shards), top_value / len(shards)))
        level = level * jnp.repeat(heights, dims[dim] // shards_of).reshape([-1 if axis == dim else 1 for axis in range(len(dims))])
    return level


def scatter_about(rng, extent, deviation, limit, pieces=(), kind=jnp.bfloat16):
    level = levels(rng, extent, pieces, -0.22, 0.18) if pieces else 1.0
    values = jax.random.normal(rng, extent, jnp.float32) * deviation * level
    return jnp.minimum(jnp.maximum(values, -limit), limit).astype(kind)


def setup_inputs(seed: int = 0) -> dict:
    streams_of = jax.random.split(jax.random.key(seed), 8)
    return {
        "pairing": draw_pairing(jax.random.fold_in(streams_of[7], 71), 0),
        "doc_start": draw_doc_start(jax.random.fold_in(streams_of[7], 71), 0),
        "block_live": draw_block_live(jax.random.fold_in(streams_of[7], 71), 0),
        "query": draw_query(jax.random.fold_in(streams_of[7], 71), 0),
        "key": draw_key(jax.random.fold_in(streams_of[7], 71), 0),
        "value": scatter_about(streams_of[5], (TOKENS, KV_HEADS * HEAD_DIM), 1.0, 6.0, ((0, 512),)),
        "grad_out": scatter_about(streams_of[6], (TOKENS, HEADS * HEAD_DIM), 1.0, 6.0, ((0, 512),)),
    }


NEGATIVE = -1.0e30


def reference(pairing, doc_start, block_live, query, key, value, grad_out):
    pair_count = pairing.shape[0]
    block_count = 2 * pair_count
    group_size = HEADS // KV_HEADS
    factor = 1.0 / (HEAD_DIM ** 0.5)
    device_ids = jnp.arange(pair_count, dtype=jnp.int32)
    global_of = jnp.stack([device_ids, (block_count - 1 - pairing).astype(jnp.int32)], axis=1).reshape(-1)
    layout_of = jnp.zeros((block_count,), jnp.int32).at[global_of].set(jnp.arange(block_count, dtype=jnp.int32))

    def to_global(source, trailing):
        return source.reshape((block_count, BLOCK) + trailing)[layout_of]

    queries = to_global(query, (KV_HEADS, group_size, HEAD_DIM))
    keys_all = to_global(key, (KV_HEADS, HEAD_DIM))
    values_all = to_global(value, (KV_HEADS, HEAD_DIM))
    cotangent = to_global(grad_out, (KV_HEADS, group_size, HEAD_DIM))
    starts_all = to_global(doc_start, ())
    padding = jnp.zeros((REACH, BLOCK, KV_HEADS, HEAD_DIM), key.dtype)
    keys_padded = jnp.concatenate([padding, keys_all], axis=0)
    values_padded = jnp.concatenate([padding, values_all], axis=0)
    offsets = jnp.arange(BLOCK, dtype=jnp.int32)
    window_ids = jnp.arange(REACH + 1, dtype=jnp.int32) - REACH

    def scores_of(position):
        key_blocks = position + window_ids
        inside = key_blocks >= 0
        clipped = jnp.clip(key_blocks, 0, block_count - 1).astype(jnp.int32)
        allowed = inside & ((key_blocks == position) | (block_live[position, clipped] == 1))
        key_places = (key_blocks[:, None] * BLOCK + offsets[None, :]).reshape(-1)
        query_places = position * BLOCK + offsets
        begins = starts_all[position]
        visible = jnp.repeat(allowed, BLOCK)[None, :] & (begins[:, None] <= key_places[None, :]) & (key_places[None, :] <= query_places[:, None])
        keys_here = lax.dynamic_slice_in_dim(keys_padded, position, REACH + 1, 0).reshape(-1, KV_HEADS, HEAD_DIM)
        values_here = lax.dynamic_slice_in_dim(values_padded, position, REACH + 1, 0).reshape(-1, KV_HEADS, HEAD_DIM)
        scores = jnp.einsum("qgrd,kgd->grqk", queries[position].astype(jnp.float32), keys_here.astype(jnp.float32)) * factor
        masked = jnp.where(visible, scores, NEGATIVE)
        return visible, masked, keys_here, values_here

    def forward(position):
        visible, masked, keys_here, values_here = scores_of(position)
        row_peak = jnp.max(masked, axis=-1)
        row_total = jnp.sum(jnp.where(visible, jnp.exp(masked - row_peak[..., None]), 0.0), axis=-1)
        logsum = row_peak + jnp.log(row_total)
        weights = jnp.where(visible, jnp.exp(masked - logsum[..., None]), 0.0).astype(jnp.bfloat16)
        weights = lax.optimization_barrier(weights).astype(jnp.float32)
        attended = jnp.einsum("grqk,kgd->qgrd", weights, values_here.astype(jnp.float32))
        return attended.astype(jnp.bfloat16), logsum

    positions = jnp.arange(block_count, dtype=jnp.int32)
    attended_all, logsum_all = lax.map(forward, positions)

    def backward(loop_state, position):
        grad_keys, grad_values = loop_state
        visible, masked, keys_here, values_here = scores_of(position)
        probabilities = jnp.where(visible, jnp.exp(masked - logsum_all[position][..., None]), 0.0)
        weights = lax.optimization_barrier(probabilities.astype(jnp.bfloat16)).astype(jnp.float32)
        upstream = cotangent[position].astype(jnp.float32)
        row_delta = jnp.einsum("qgrd,qgrd->grq", upstream, attended_all[position].astype(jnp.float32))
        dweights = jnp.einsum("qgrd,kgd->grqk", upstream, values_here.astype(jnp.float32))
        dscores = lax.optimization_barrier((probabilities * (dweights - row_delta[..., None])).astype(jnp.bfloat16)).astype(jnp.float32)
        query_block_grad = (jnp.einsum("grqk,kgd->qgrd", dscores, keys_here.astype(jnp.float32)) * factor).astype(jnp.bfloat16)
        key_part = jnp.einsum("grqk,qgrd->kgd", dscores, queries[position].astype(jnp.float32)) * factor
        value_part = jnp.einsum("grqk,qgrd->kgd", weights, upstream)
        window_rows = (REACH + 1) * BLOCK
        first_row = position * BLOCK
        grad_keys = lax.dynamic_update_slice_in_dim(grad_keys, lax.dynamic_slice_in_dim(grad_keys, first_row, window_rows, 0) + key_part, first_row, 0)
        grad_values = lax.dynamic_update_slice_in_dim(grad_values, lax.dynamic_slice_in_dim(grad_values, first_row, window_rows, 0) + value_part, first_row, 0)
        return (grad_keys, grad_values), query_block_grad

    zeros_grad = jnp.zeros(((block_count + REACH) * BLOCK, KV_HEADS, HEAD_DIM), jnp.float32)
    (grad_keys, grad_values), query_grads = lax.scan(backward, (zeros_grad, zeros_grad), positions)
    total_rows = block_count * BLOCK
    attended_out = attended_all[global_of].reshape(total_rows, HEADS * HEAD_DIM)
    query_out = query_grads[global_of].reshape(total_rows, HEADS * HEAD_DIM)
    key_out = grad_keys[REACH * BLOCK:].reshape(block_count, BLOCK, KV_HEADS * HEAD_DIM)[global_of].reshape(total_rows, KV_HEADS * HEAD_DIM)
    value_out = grad_values[REACH * BLOCK:].reshape(block_count, BLOCK, KV_HEADS * HEAD_DIM)[global_of].reshape(total_rows, KV_HEADS * HEAD_DIM)
    return attended_out, query_out, key_out.astype(jnp.bfloat16), value_out.astype(jnp.bfloat16)
```

```python
import functools
import math

import jax
import jax.numpy as jnp
from jax import lax
from jax.experimental import pallas as pl
from jax.experimental.pallas import tpu as pltpu
from jax.sharding import Mesh
from jax.sharding import PartitionSpec as P

DIM = 128
BLOCK = 128
REACH = 4
WINDOW = REACH + 1
GROUP = 4
PARTS = 8
ROWS = 2 * BLOCK
PIECE = ROWS // PARTS
SLOTS = 8
NEGATIVE = -1e30
QUERY_WIDE = GROUP * DIM
KEY_AT = 2 * QUERY_WIDE
WIDE = KEY_AT + 2 * DIM
SENT = WIDE + DIM


def dot(a, b, over_a, over_b):
    return lax.dot_general(
        a, b, (((over_a,), (over_b,)), ((), ())), preferred_element_type=jnp.float32
    )


def pieces(whole, split, at, wide):
    return [
        (whole.at[:, pl.ds(h * wide, wide)], split.at[h, :, pl.ds(at, wide)]) for h in range(PARTS)
    ]


def places(q, g, k, v, split):
    return (
        pieces(q, split, 0, QUERY_WIDE)
        + pieces(g, split, QUERY_WIDE, QUERY_WIDE)
        + pieces(k, split, KEY_AT, DIM)
        + pieces(v, split, KEY_AT + DIM, DIM)
    )


def pack_kernel(doc_ref, q_ref, g_ref, k_ref, v_ref, out_ref, doc_here, sems, doc_sem):
    doc_copy = pltpu.make_async_copy(doc_ref, doc_here, doc_sem)
    doc_copy.start()
    copies = [
        pltpu.make_async_copy(rows, split, sems.at[i])
        for i, (rows, split) in enumerate(places(q_ref, g_ref, k_ref, v_ref, out_ref))
    ]
    for copy in copies:
        copy.start()
    doc_copy.wait()
    doc = doc_here[...]
    line = lax.broadcasted_iota(jnp.int32, (PIECE, BLOCK), 0)
    first, second = doc[:, :BLOCK], doc[:, BLOCK:]
    coded = jnp.where(line < 2, first, second)
    coded = jnp.where(line % 2 == 0, coded // BLOCK, coded % BLOCK)
    coded = coded.astype(jnp.float32).astype(jnp.bfloat16)
    for h in range(PARTS):
        out_ref[h, :, WIDE:] = coded
    for copy in copies:
        copy.wait()


def pack(doc, query, grad_out, key, value):
    vmem = pl.BlockSpec(memory_space=pltpu.VMEM)
    hbm = pl.BlockSpec(memory_space=pltpu.HBM)
    return pl.pallas_call(
        pack_kernel,
        out_shape=jax.ShapeDtypeStruct((PARTS, PIECE, SENT), jnp.bfloat16),
        in_specs=[hbm] * 5,
        out_specs=vmem,
        scratch_shapes=[
            pltpu.VMEM((1, ROWS), jnp.int32),
            pltpu.SemaphoreType.DMA((4 * PARTS,)),
            pltpu.SemaphoreType.DMA,
        ],
        compiler_params=pltpu.CompilerParams(vmem_limit_bytes=(63 * 1024 + 256) * 1024),
        name="pack",
    )(doc, query, grad_out, key, value)


def unpack_kernel(split_ref, att_ref, dq_ref, dk_ref, dv_ref, sems):
    copies = [
        pltpu.make_async_copy(split, rows, sems.at[i])
        for i, (rows, split) in enumerate(places(att_ref, dq_ref, dk_ref, dv_ref, split_ref))
    ]
    for copy in copies:
        copy.start()
    for copy in copies:
        copy.wait()


def unpack(split):
    hbm = pl.BlockSpec(memory_space=pltpu.HBM)
    wide = jax.ShapeDtypeStruct((PIECE, PARTS * QUERY_WIDE), jnp.bfloat16)
    narrow = jax.ShapeDtypeStruct((PIECE, PARTS * DIM), jnp.bfloat16)
    return pl.pallas_call(
        unpack_kernel,
        out_shape=(wide, wide, narrow, narrow),
        in_specs=[pl.BlockSpec(memory_space=pl.ANY)],
        out_specs=(hbm,) * 4,
        scratch_shapes=[pltpu.SemaphoreType.DMA((4 * PARTS,))],
        compiler_params=pltpu.CompilerParams(vmem_limit_bytes=16 * 1024 * 1024),
        name="unpack",
    )(split)


def gather_kernel(
    place_ref, pairing_ref, od_ref, own_ref, one_ref, two_ref, three_ref, back_ref, out_ref
):
    pair = place_ref[0]
    later = (place_ref[2] == 0) | (pairing_ref[2 * pair + 1] < pairing_ref[2 * pair])
    out_ref[:, :KEY_AT] = od_ref[...]
    total = own_ref[...] + one_ref[...].astype(jnp.float32) + two_ref[...].astype(jnp.float32)
    three = three_ref[...].astype(jnp.float32)
    lower = total[:BLOCK] + jnp.where(later, 0.0, three)
    upper = total[BLOCK:] + jnp.where(later, three, 0.0) + back_ref[...].astype(jnp.float32)
    out_ref[:BLOCK, KEY_AT:] = lower.astype(jnp.bfloat16)
    out_ref[BLOCK:, KEY_AT:] = upper.astype(jnp.bfloat16)


def gather(place, pairing, od, parts):
    vmem = pl.BlockSpec(memory_space=pltpu.VMEM)
    smem = pl.BlockSpec(memory_space=pltpu.SMEM)
    return pl.pallas_call(
        gather_kernel,
        out_shape=jax.ShapeDtypeStruct((ROWS, WIDE), jnp.bfloat16),
        in_specs=[smem, smem] + [vmem] * 6,
        out_specs=vmem,
        compiler_params=pltpu.CompilerParams(vmem_limit_bytes=16 * 1024 * 1024),
        name="gather",
    )(place, pairing, od, *parts)


def attention_kernel(
    chain,
    place_ref,
    pairing_ref,
    live_ref,
    qg_ref,
    one_ref,
    two_ref,
    three_ref,
    back_ref,
    od_ref,
    own_out,
    one_out,
    two_out,
    three_out,
    back_out,
    kv,
    acc,
):
    pair = place_ref[0]
    half = place_ref[2]
    blocks = 2 * chain
    ctx = chain
    scale = 1.0 / math.sqrt(DIM)
    my_place = jnp.where(half == 0, pair, chain - 1 - pair)

    kv[0:256, :] = qg_ref[:, KEY_AT:WIDE]
    kv[256:512, :] = one_ref[...]
    kv[512:768, :] = two_ref[...]
    kv[768:896, :] = three_ref[...]
    kv[896:1024, :] = back_ref[...]
    acc[...] = jnp.zeros_like(acc)

    keys_down = lax.broadcasted_iota(jnp.int32, (BLOCK, BLOCK), 0)
    rows_along = lax.broadcasted_iota(jnp.int32, (BLOCK, BLOCK), 1)
    lanes = lax.broadcasted_iota(jnp.int32, (1, blocks), 1)

    for b in range(2):
        holder = 2 * pair + b
        block = jnp.where(half == 0, holder, blocks - 1 - pairing_ref[holder])
        doc = qg_ref[b * BLOCK : b * BLOCK + PIECE, WIDE:].astype(jnp.float32)
        doc = jnp.where(half == 0, doc[0:2], doc[2:4])
        begins = (doc[0:1] * BLOCK + doc[1:2]).astype(jnp.int32)
        live_row = live_ref[pl.ds(block, 1), :]
        slots = []
        bias = []
        for w in range(WINDOW):
            key_block = block - w
            mirrored = pairing_ref[jnp.clip(blocks - 1 - key_block, 0, ctx - 1)]
            held_by = jnp.where(key_block < ctx, key_block, mirrored)
            where_held = jnp.where(key_block < ctx, held_by // 2, chain - 1 - held_by // 2)
            away = my_place - where_held
            slot = jnp.where(away == 3, 6, jnp.where(away == -1, 7, 2 * away + held_by % 2))
            slot = jnp.where(key_block >= 0, jnp.clip(slot, 0, SLOTS - 1), 0)
            slots.append(pl.multiple_of(slot * BLOCK, BLOCK))
            reach = begins - key_block * BLOCK
            if w == 0:
                seen = (keys_down >= reach) & (keys_down <= rows_along)
            else:
                listed = jnp.max(
                    jnp.where(lanes == key_block, live_row, 0), axis=1, keepdims=True
                )
                seen = keys_down >= jnp.where(listed == 1, reach, BLOCK)
            bias.append(jnp.where(seen, 0.0, NEGATIVE))
        bias = jnp.concatenate(bias, axis=0)
        bias = jnp.concatenate([bias, bias], axis=1)
        keys = jnp.concatenate([kv[pl.ds(s, BLOCK), :DIM] for s in slots], axis=0)
        values = jnp.concatenate([kv[pl.ds(s, BLOCK), DIM:] for s in slots], axis=0)
        rows = slice(b * BLOCK, (b + 1) * BLOCK)
        key_grad = None
        value_grad = None
        for h in range(0, GROUP, 2):
            first, second = h * DIM, (h + 1) * DIM
            shift = GROUP * DIM
            q = jnp.concatenate(
                [qg_ref[rows, first : first + DIM], qg_ref[rows, second : second + DIM]], axis=0
            )
            g = jnp.concatenate(
                [
                    qg_ref[rows, shift + first : shift + first + DIM],
                    qg_ref[rows, shift + second : shift + second + DIM],
                ],
                axis=0,
            )
            scores = dot(keys, q, 1, 1) + bias
            peak = jnp.max(scores, axis=0, keepdims=True)
            p = jnp.exp2((scores - peak) * (scale * math.log2(math.e)))
            p = p * (1.0 / jnp.sum(p, axis=0, keepdims=True))
            weights = p.astype(jnp.bfloat16)
            out = dot(values, weights, 0, 0)
            g_turned = g.astype(jnp.float32).T
            delta = jnp.sum(
                g_turned * out.astype(jnp.bfloat16).astype(jnp.float32), axis=0, keepdims=True
            )
            dweights = dot(values, g, 1, 1)
            dscores = (p * (dweights - delta)).astype(jnp.bfloat16)
            dq = dot(keys, dscores, 0, 0) * scale
            key_new = dot(dscores, q, 1, 0)
            value_new = dot(weights, g, 1, 0)
            key_grad = key_new if key_grad is None else key_grad + key_new
            value_grad = value_new if value_grad is None else value_grad + value_new
            out = out.T.astype(jnp.bfloat16)
            dq = dq.T.astype(jnp.bfloat16)
            od_ref[rows, first : first + DIM] = out[:BLOCK]
            od_ref[rows, second : second + DIM] = out[BLOCK:]
            od_ref[rows, shift + first : shift + first + DIM] = dq[:BLOCK]
            od_ref[rows, shift + second : shift + second + DIM] = dq[BLOCK:]
        key_grad = key_grad * scale
        for w, s in enumerate(slots):
            part = slice(w * BLOCK, (w + 1) * BLOCK)
            acc[pl.ds(s, BLOCK), :DIM] += key_grad[part]
            acc[pl.ds(s, BLOCK), DIM:] += value_grad[part]

    own_out[...] = acc[0:256, :]
    one_out[...] = acc[256:512, :].astype(jnp.bfloat16)
    two_out[...] = acc[512:768, :].astype(jnp.bfloat16)
    three_out[...] = acc[768:896, :].astype(jnp.bfloat16)
    back_out[...] = acc[896:1024, :].astype(jnp.bfloat16)


def attention(chain, place, pairing, live, qg, halo):
    wide = 2 * DIM
    vmem = pl.BlockSpec(memory_space=pltpu.VMEM)
    smem = pl.BlockSpec(memory_space=pltpu.SMEM)
    return pl.pallas_call(
        functools.partial(attention_kernel, chain),
        out_shape=(
            jax.ShapeDtypeStruct((ROWS, 2 * GROUP * DIM), jnp.bfloat16),
            jax.ShapeDtypeStruct((ROWS, wide), jnp.float32),
            jax.ShapeDtypeStruct((ROWS, wide), jnp.bfloat16),
            jax.ShapeDtypeStruct((ROWS, wide), jnp.bfloat16),
            jax.ShapeDtypeStruct((BLOCK, wide), jnp.bfloat16),
            jax.ShapeDtypeStruct((BLOCK, wide), jnp.bfloat16),
        ),
        in_specs=[smem, smem] + [vmem] * 6,
        out_specs=(vmem,) * 6,
        scratch_shapes=[
            pltpu.VMEM((SLOTS * BLOCK, wide), jnp.bfloat16),
            pltpu.VMEM((SLOTS * BLOCK, wide), jnp.float32),
        ],
        compiler_params=pltpu.CompilerParams(vmem_limit_bytes=32 * 1024 * 1024),
        cost_estimate=pl.CostEstimate(
            flops=2 * 5 * 2 * WINDOW * GROUP * BLOCK * BLOCK * DIM,
            bytes_accessed=3 * 1024 * 1024,
            transcendentals=2 * WINDOW * GROUP * BLOCK * BLOCK,
        ),
        name="attention",
    )(place, pairing, live, qg, *halo)


def body(pairing, doc_start, block_live, query, key, value, grad_out):
    pairs = lax.axis_size("pair")
    chain = 2 * pairs
    blocks = 2 * chain
    pair = lax.axis_index("pair")
    side = lax.axis_index("side")
    half = lax.axis_index("half")

    def linear(place):
        return place * 2 if place < pairs else (chain - 1 - place) * 2 + 1

    def steps(by, first_target):
        return [
            (linear(s - by), linear(s)) for s in range(first_target, chain) if 0 <= s - by < chain
        ]

    forth = [steps(1, 0), steps(2, 0), steps(3, pairs), steps(-1, pairs)]
    back = [[(b, a) for a, b in pairs_of] for pairs_of in forth]

    def move(x, pairs_of):
        return lax.ppermute(x, ("pair", "half"), pairs_of)

    def exchange(x):
        return lax.all_to_all(x, ("side", "lane"), split_axis=0, concat_axis=0, tiled=True)

    split = pack(doc_start.reshape(1, ROWS), query, grad_out, key, value)
    arrived = exchange(split).reshape(ROWS, SENT)
    own = arrived[:, KEY_AT:WIDE]
    later = (half == 0) | (pairing[2 * pair + 1] < pairing[2 * pair])
    halo = (
        move(own, forth[0]),
        move(own, forth[1]),
        move(jnp.where(later, own[BLOCK:], own[:BLOCK]), forth[2]),
        move(own[BLOCK:], forth[3]),
    )
    place = jnp.stack([pair, side, half]).astype(jnp.int32)
    od, own_grad, *partials = attention(chain, place, pairing, block_live, arrived, halo)
    partials = [move(part, pairs_of) for part, pairs_of in zip(partials, back)]
    total = gather(place, pairing, od, (own_grad, *partials))
    return unpack(exchange(total.reshape(PARTS, PIECE, WIDE)))


def solution(mesh):
    ctx, head = mesh.devices.shape
    fine = Mesh(mesh.devices.reshape(ctx // 2, 2, 2, head // 2), ("pair", "side", "half", "lane"))
    tokens = P(("pair", "side", "half", "lane"), None)
    return jax.shard_map(
        body,
        mesh=fine,
        in_specs=(P(), P(("pair", "side")), P(), tokens, tokens, tokens, tokens),
        out_specs=(tokens,) * 4,
        check_vma=False,
    )
```

```python
import functools
import math

import jax
import jax.numpy as jnp
from jax import lax
from jax.experimental import pallas as pl
from jax.experimental.pallas import tpu as pltpu
from jax.sharding import Mesh
from jax.sharding import PartitionSpec as P

DIM = 128
BLOCK = 128
REACH = 4
WINDOW = REACH + 1
GROUP = 4
PARTS = 8
ROWS = 2 * BLOCK
PIECE = ROWS // PARTS
SLOTS = 8
NEGATIVE = -1e30
QUERY_WIDE = GROUP * DIM
QG_WIDE = 2 * QUERY_WIDE


def dot(a, b, over_a, over_b):
    return lax.dot_general(
        a, b, (((over_a,), (over_b,)), ((), ())), preferred_element_type=jnp.float32
    )


def pieces(whole, split, at, wide):
    return [
        (whole.at[:, pl.ds(h * wide, wide)], split.at[h, :, pl.ds(at, wide)]) for h in range(PARTS)
    ]


def copies_of(first, second, split, at, wide, sems, cut):
    pairs = pieces(first, split, at, wide) + pieces(second, split, at + wide, wide)
    return [
        pltpu.make_async_copy(*((rows, piece) if cut else (piece, rows)), sems.at[i])
        for i, (rows, piece) in enumerate(pairs)
    ]


def pack_kernel(wide, first_ref, second_ref, *refs):
    if len(refs) == 2:
        out_ref, sems = refs
    else:
        doc_ref, out_ref, sems, doc_here, doc_sem = refs
        doc_copy = pltpu.make_async_copy(doc_ref, doc_here, doc_sem)
        doc_copy.start()
    copies = copies_of(first_ref, second_ref, out_ref, 0, wide, sems, True)
    for copy in copies:
        copy.start()
    if len(refs) > 2:
        doc_copy.wait()
        doc = doc_here[...]
        line = lax.broadcasted_iota(jnp.int32, (PIECE, BLOCK), 0)
        coded = jnp.where(line < 2, doc[:, :BLOCK], doc[:, BLOCK:])
        coded = jnp.where(line % 2 == 0, coded // BLOCK, coded % BLOCK)
        coded = coded.astype(jnp.float32).astype(jnp.bfloat16)
        for h in range(PARTS):
            out_ref[h, :, 2 * wide :] = coded
    for copy in copies:
        copy.wait()


def pack(first, second, doc=None):
    hbm = pl.BlockSpec(memory_space=pltpu.HBM)
    wide = first.shape[1] // PARTS
    scratch = [pltpu.SemaphoreType.DMA((2 * PARTS,))]
    arrays = (first, second)
    sent = 2 * wide
    if doc is not None:
        scratch += [pltpu.VMEM((1, ROWS), jnp.int32), pltpu.SemaphoreType.DMA]
        arrays += (doc,)
        sent += DIM
    return pl.pallas_call(
        functools.partial(pack_kernel, wide),
        out_shape=jax.ShapeDtypeStruct((PARTS, PIECE, sent), jnp.bfloat16),
        in_specs=[hbm] * len(arrays),
        out_specs=pl.BlockSpec(memory_space=pltpu.VMEM),
        scratch_shapes=scratch,
        compiler_params=pltpu.CompilerParams(vmem_limit_bytes=(63 * 1024 + 256) * 1024),
        name="pack",
    )(*arrays)


def unpack_kernel(split_ref, att_ref, dq_ref, dk_ref, dv_ref, sems):
    copies = copies_of(att_ref, dq_ref, split_ref, 0, QUERY_WIDE, sems, False)
    copies += copies_of(dk_ref, dv_ref, split_ref, QG_WIDE, DIM, sems.at[2 * PARTS :], False)
    for copy in copies:
        copy.start()
    for copy in copies:
        copy.wait()


def unpack(split):
    hbm = pl.BlockSpec(memory_space=pltpu.HBM)
    wide = jax.ShapeDtypeStruct((PIECE, PARTS * QUERY_WIDE), jnp.bfloat16)
    narrow = jax.ShapeDtypeStruct((PIECE, PARTS * DIM), jnp.bfloat16)
    return pl.pallas_call(
        unpack_kernel,
        out_shape=(wide, wide, narrow, narrow),
        in_specs=[pl.BlockSpec(memory_space=pl.ANY)],
        out_specs=(hbm,) * 4,
        scratch_shapes=[pltpu.SemaphoreType.DMA((4 * PARTS,))],
        compiler_params=pltpu.CompilerParams(vmem_limit_bytes=16 * 1024 * 1024),
        name="unpack",
    )(split)


def gather_kernel(
    place_ref, pairing_ref, od_ref, own_ref, one_ref, two_ref, three_ref, back_ref, out_ref
):
    pair = place_ref[0]
    later = (place_ref[2] == 0) | (pairing_ref[2 * pair + 1] < pairing_ref[2 * pair])
    out_ref[:, :QG_WIDE] = od_ref[...]
    total = own_ref[...] + one_ref[...].astype(jnp.float32) + two_ref[...].astype(jnp.float32)
    three = three_ref[...].astype(jnp.float32)
    lower = total[:BLOCK] + jnp.where(later, 0.0, three)
    upper = total[BLOCK:] + jnp.where(later, three, 0.0) + back_ref[...].astype(jnp.float32)
    out_ref[:BLOCK, QG_WIDE:] = lower.astype(jnp.bfloat16)
    out_ref[BLOCK:, QG_WIDE:] = upper.astype(jnp.bfloat16)


def gather(place, pairing, od, parts):
    vmem = pl.BlockSpec(memory_space=pltpu.VMEM)
    smem = pl.BlockSpec(memory_space=pltpu.SMEM)
    return pl.pallas_call(
        gather_kernel,
        out_shape=jax.ShapeDtypeStruct((ROWS, QG_WIDE + 2 * DIM), jnp.bfloat16),
        in_specs=[smem, smem] + [vmem] * 6,
        out_specs=vmem,
        compiler_params=pltpu.CompilerParams(vmem_limit_bytes=16 * 1024 * 1024),
        name="gather",
    )(place, pairing, od, *parts)


def attention_kernel(
    chain,
    place_ref,
    pairing_ref,
    live_ref,
    qg_ref,
    own_ref,
    one_ref,
    two_ref,
    three_ref,
    back_ref,
    od_ref,
    own_out,
    one_out,
    two_out,
    three_out,
    back_out,
    kv,
    acc,
):
    pair = place_ref[0]
    half = place_ref[2]
    blocks = 2 * chain
    ctx = chain
    scale = 1.0 / math.sqrt(DIM)
    my_place = jnp.where(half == 0, pair, chain - 1 - pair)

    kv[0:256, :] = own_ref[...]
    kv[256:512, :] = one_ref[...]
    kv[512:768, :] = two_ref[...]
    kv[768:896, :] = three_ref[...]
    kv[896:1024, :] = back_ref[...]
    acc[...] = jnp.zeros_like(acc)

    keys_down = lax.broadcasted_iota(jnp.int32, (BLOCK, BLOCK), 0)
    rows_along = lax.broadcasted_iota(jnp.int32, (BLOCK, BLOCK), 1)
    lanes = lax.broadcasted_iota(jnp.int32, (1, blocks), 1)

    for b in range(2):
        holder = 2 * pair + b
        block = jnp.where(half == 0, holder, blocks - 1 - pairing_ref[holder])
        doc = qg_ref[b * BLOCK : b * BLOCK + PIECE, QG_WIDE:].astype(jnp.float32)
        doc = jnp.where(half == 0, doc[0:2], doc[2:4])
        begins = (doc[0:1] * BLOCK + doc[1:2]).astype(jnp.int32)
        live_row = live_ref[pl.ds(block, 1), :]
        slots = []
        bias = []
        for w in range(WINDOW):
            key_block = block - w
            mirrored = pairing_ref[jnp.clip(blocks - 1 - key_block, 0, ctx - 1)]
            held_by = jnp.where(key_block < ctx, key_block, mirrored)
            where_held = jnp.where(key_block < ctx, held_by // 2, chain - 1 - held_by // 2)
            away = my_place - where_held
            slot = jnp.where(away == 3, 6, jnp.where(away == -1, 7, 2 * away + held_by % 2))
            slot = jnp.where(key_block >= 0, jnp.clip(slot, 0, SLOTS - 1), 0)
            slots.append(pl.multiple_of(slot * BLOCK, BLOCK))
            reach = begins - key_block * BLOCK
            if w == 0:
                seen = (keys_down >= reach) & (keys_down <= rows_along)
            else:
                listed = jnp.max(
                    jnp.where(lanes == key_block, live_row, 0), axis=1, keepdims=True
                )
                seen = keys_down >= jnp.where(listed == 1, reach, BLOCK)
            bias.append(jnp.where(seen, 0.0, NEGATIVE))
        bias = jnp.concatenate(bias, axis=0)
        bias = jnp.concatenate([bias, bias], axis=1)
        keys = jnp.concatenate([kv[pl.ds(s, BLOCK), :DIM] for s in slots], axis=0)
        values = jnp.concatenate([kv[pl.ds(s, BLOCK), DIM:] for s in slots], axis=0)
        rows = slice(b * BLOCK, (b + 1) * BLOCK)
        key_grad = None
        value_grad = None
        for h in range(0, GROUP, 2):
            first, second = h * DIM, (h + 1) * DIM
            shift = GROUP * DIM
            q = jnp.concatenate(
                [qg_ref[rows, first : first + DIM], qg_ref[rows, second : second + DIM]], axis=0
            )
            g = jnp.concatenate(
                [
                    qg_ref[rows, shift + first : shift + first + DIM],
                    qg_ref[rows, shift + second : shift + second + DIM],
                ],
                axis=0,
            )
            scores = dot(keys, q, 1, 1) + bias
            peak = jnp.max(scores, axis=0, keepdims=True)
            p = jnp.exp2((scores - peak) * (scale * math.log2(math.e)))
            p = p * (1.0 / jnp.sum(p, axis=0, keepdims=True))
            weights = p.astype(jnp.bfloat16)
            out = dot(values, weights, 0, 0)
            g_turned = g.astype(jnp.float32).T
            delta = jnp.sum(
                g_turned * out.astype(jnp.bfloat16).astype(jnp.float32), axis=0, keepdims=True
            )
            dweights = dot(values, g, 1, 1)
            dscores = (p * (dweights - delta)).astype(jnp.bfloat16)
            dq = dot(keys, dscores, 0, 0) * scale
            key_new = dot(dscores, q, 1, 0)
            value_new = dot(weights, g, 1, 0)
            key_grad = key_new if key_grad is None else key_grad + key_new
            value_grad = value_new if value_grad is None else value_grad + value_new
            out = out.T.astype(jnp.bfloat16)
            dq = dq.T.astype(jnp.bfloat16)
            od_ref[rows, first : first + DIM] = out[:BLOCK]
            od_ref[rows, second : second + DIM] = out[BLOCK:]
            od_ref[rows, shift + first : shift + first + DIM] = dq[:BLOCK]
            od_ref[rows, shift + second : shift + second + DIM] = dq[BLOCK:]
        key_grad = key_grad * scale
        for w, s in enumerate(slots):
            part = slice(w * BLOCK, (w + 1) * BLOCK)
            acc[pl.ds(s, BLOCK), :DIM] += key_grad[part]
            acc[pl.ds(s, BLOCK), DIM:] += value_grad[part]

    own_out[...] = acc[0:256, :]
    one_out[...] = acc[256:512, :].astype(jnp.bfloat16)
    two_out[...] = acc[512:768, :].astype(jnp.bfloat16)
    three_out[...] = acc[768:896, :].astype(jnp.bfloat16)
    back_out[...] = acc[896:1024, :].astype(jnp.bfloat16)


def attention(chain, place, pairing, live, qg, halo):
    wide = 2 * DIM
    vmem = pl.BlockSpec(memory_space=pltpu.VMEM)
    smem = pl.BlockSpec(memory_space=pltpu.SMEM)
    return pl.pallas_call(
        functools.partial(attention_kernel, chain),
        out_shape=(
            jax.ShapeDtypeStruct((ROWS, 2 * GROUP * DIM), jnp.bfloat16),
            jax.ShapeDtypeStruct((ROWS, wide), jnp.float32),
            jax.ShapeDtypeStruct((ROWS, wide), jnp.bfloat16),
            jax.ShapeDtypeStruct((ROWS, wide), jnp.bfloat16),
            jax.ShapeDtypeStruct((BLOCK, wide), jnp.bfloat16),
            jax.ShapeDtypeStruct((BLOCK, wide), jnp.bfloat16),
        ),
        in_specs=[smem, smem] + [vmem] * 7,
        out_specs=(vmem,) * 6,
        scratch_shapes=[
            pltpu.VMEM((SLOTS * BLOCK, wide), jnp.bfloat16),
            pltpu.VMEM((SLOTS * BLOCK, wide), jnp.float32),
        ],
        compiler_params=pltpu.CompilerParams(vmem_limit_bytes=32 * 1024 * 1024),
        cost_estimate=pl.CostEstimate(
            flops=2 * 5 * 2 * WINDOW * GROUP * BLOCK * BLOCK * DIM,
            bytes_accessed=3 * 1024 * 1024,
            transcendentals=2 * WINDOW * GROUP * BLOCK * BLOCK,
        ),
        name="attention",
    )(place, pairing, live, qg, *halo)


def body(pairing, doc_start, block_live, query, key, value, grad_out):
    pairs = lax.axis_size("pair")
    chain = 2 * pairs
    blocks = 2 * chain
    pair = lax.axis_index("pair")
    side = lax.axis_index("side")
    half = lax.axis_index("half")

    def linear(place):
        return place * 2 if place < pairs else (chain - 1 - place) * 2 + 1

    def steps(by, first_target):
        return [
            (linear(s - by), linear(s)) for s in range(first_target, chain) if 0 <= s - by < chain
        ]

    forth = [steps(1, 0), steps(2, 0), steps(3, pairs), steps(-1, pairs)]
    back = [[(b, a) for a, b in pairs_of] for pairs_of in forth]

    def move(x, pairs_of):
        return lax.ppermute(x, ("pair", "half"), pairs_of)

    def exchange(x):
        return lax.all_to_all(x, ("side", "lane"), split_axis=0, concat_axis=0, tiled=True)

    later = (half == 0) | (pairing[2 * pair + 1] < pairing[2 * pair])
    own = exchange(pack(key, value)).reshape(ROWS, 2 * DIM)
    split, later = lax.optimization_barrier(
        (pack(query, grad_out, doc_start.reshape(1, ROWS)), later)
    )
    split, own = lax.optimization_barrier((split, own))
    qg = exchange(split).reshape(ROWS, QG_WIDE + DIM)
    halo = (
        own,
        move(own, forth[0]),
        move(own, forth[1]),
        move(jnp.where(later, own[BLOCK:], own[:BLOCK]), forth[2]),
        move(own[BLOCK:], forth[3]),
    )
    place = jnp.stack([pair, side, half]).astype(jnp.int32)
    od, own_grad, *partials = attention(chain, place, pairing, block_live, qg, halo)
    partials = [move(part, pairs_of) for part, pairs_of in zip(partials, back)]
    total = gather(place, pairing, od, (own_grad, *partials))
    return unpack(exchange(total.reshape(PARTS, PIECE, -1)))


def solution(mesh):
    ctx, head = mesh.devices.shape
    fine = Mesh(mesh.devices.reshape(ctx // 2, 2, 2, head // 2), ("pair", "side", "half", "lane"))
    tokens = P(("pair", "side", "half", "lane"), None)
    return jax.shard_map(
        body,
        mesh=fine,
        in_specs=(P(), P(("pair", "side")), P(), tokens, tokens, tokens, tokens),
        out_specs=(tokens,) * 4,
        check_vma=False,
    )
```

```python
import functools
import math

import jax
import jax.numpy as jnp
from jax import lax
from jax.experimental import pallas as pl
from jax.experimental.pallas import tpu as pltpu
from jax.sharding import Mesh
from jax.sharding import PartitionSpec as P

DIM = 128
BLOCK = 128
REACH = 4
WINDOW = REACH + 1
GROUP = 4
PARTS = 8
ROWS = 2 * BLOCK
PIECE = ROWS // PARTS
NEGATIVE = -1e30
QUERY_WIDE = GROUP * DIM
QG_WIDE = 2 * QUERY_WIDE


def dot(a, b, over_a, over_b):
    return lax.dot_general(
        a, b, (((over_a,), (over_b,)), ((), ())), preferred_element_type=jnp.float32
    )


def pieces(whole, split, at, wide):
    return [
        (whole.at[:, pl.ds(h * wide, wide)], split.at[h, :, pl.ds(at, wide)]) for h in range(PARTS)
    ]


def copies_of(first, second, split, at, wide, sems, cut):
    pairs = pieces(first, split, at, wide) + pieces(second, split, at + wide, wide)
    return [
        pltpu.make_async_copy(*((rows, piece) if cut else (piece, rows)), sems.at[i])
        for i, (rows, piece) in enumerate(pairs)
    ]


def pack_kernel(wide, first_ref, second_ref, *refs):
    if len(refs) == 2:
        out_ref, sems = refs
    else:
        doc_ref, out_ref, sems, doc_here, doc_sem = refs
        doc_copy = pltpu.make_async_copy(doc_ref, doc_here, doc_sem)
        doc_copy.start()
    copies = copies_of(first_ref, second_ref, out_ref, 0, wide, sems, True)
    for copy in copies:
        copy.start()
    if len(refs) > 2:
        doc_copy.wait()
        doc = doc_here[...]
        line = lax.broadcasted_iota(jnp.int32, (PIECE, BLOCK), 0)
        coded = jnp.where(line < 2, doc[:, :BLOCK], doc[:, BLOCK:])
        coded = jnp.where(line % 2 == 0, coded // BLOCK, coded % BLOCK)
        coded = coded.astype(jnp.float32).astype(jnp.bfloat16)
        for h in range(PARTS):
            out_ref[h, :, 2 * wide :] = coded
    for copy in copies:
        copy.wait()


def pack(first, second, doc=None):
    hbm = pl.BlockSpec(memory_space=pltpu.HBM)
    wide = first.shape[1] // PARTS
    scratch = [pltpu.SemaphoreType.DMA((2 * PARTS,))]
    arrays = (first, second)
    sent = 2 * wide
    if doc is not None:
        scratch += [pltpu.VMEM((1, ROWS), jnp.int32), pltpu.SemaphoreType.DMA]
        arrays += (doc,)
        sent += DIM
    return pl.pallas_call(
        functools.partial(pack_kernel, wide),
        out_shape=jax.ShapeDtypeStruct((PARTS, PIECE, sent), jnp.bfloat16),
        in_specs=[hbm] * len(arrays),
        out_specs=pl.BlockSpec(memory_space=pltpu.VMEM),
        scratch_shapes=scratch,
        compiler_params=pltpu.CompilerParams(vmem_limit_bytes=(63 * 1024 + 256) * 1024),
        name="pack",
    )(*arrays)


def unpack_kernel(split_ref, att_ref, dq_ref, dk_ref, dv_ref, sems):
    copies = copies_of(att_ref, dq_ref, split_ref, 0, QUERY_WIDE, sems, False)
    copies += copies_of(dk_ref, dv_ref, split_ref, QG_WIDE, DIM, sems.at[2 * PARTS :], False)
    for copy in copies:
        copy.start()
    for copy in copies:
        copy.wait()


def unpack(split):
    hbm = pl.BlockSpec(memory_space=pltpu.HBM)
    wide = jax.ShapeDtypeStruct((PIECE, PARTS * QUERY_WIDE), jnp.bfloat16)
    narrow = jax.ShapeDtypeStruct((PIECE, PARTS * DIM), jnp.bfloat16)
    return pl.pallas_call(
        unpack_kernel,
        out_shape=(wide, wide, narrow, narrow),
        in_specs=[pl.BlockSpec(memory_space=pl.ANY)],
        out_specs=(hbm,) * 4,
        scratch_shapes=[pltpu.SemaphoreType.DMA((4 * PARTS,))],
        compiler_params=pltpu.CompilerParams(vmem_limit_bytes=16 * 1024 * 1024),
        name="unpack",
    )(split)


def gather_kernel(place_ref, pairing_ref, od_ref, own_ref, one_ref, two_ref, *refs):
    *extra, out_ref = refs
    out_ref[:, :QG_WIDE] = od_ref[...]
    total = own_ref[...] + one_ref[...].astype(jnp.float32) + two_ref[...].astype(jnp.float32)
    lower, upper = total[:BLOCK], total[BLOCK:]
    if extra:
        three_ref, back_ref = extra
        pair = place_ref[0]
        later = (place_ref[2] == 0) | (pairing_ref[2 * pair + 1] < pairing_ref[2 * pair])
        three = three_ref[...].astype(jnp.float32)
        lower = lower + jnp.where(later, 0.0, three)
        upper = upper + jnp.where(later, three, 0.0) + back_ref[...].astype(jnp.float32)
    out_ref[:BLOCK, QG_WIDE:] = lower.astype(jnp.bfloat16)
    out_ref[BLOCK:, QG_WIDE:] = upper.astype(jnp.bfloat16)


def gather(place, pairing, od, parts):
    vmem = pl.BlockSpec(memory_space=pltpu.VMEM)
    smem = pl.BlockSpec(memory_space=pltpu.SMEM)
    return pl.pallas_call(
        gather_kernel,
        out_shape=jax.ShapeDtypeStruct((ROWS, QG_WIDE + 2 * DIM), jnp.bfloat16),
        in_specs=[smem, smem] + [vmem] * (1 + len(parts)),
        out_specs=vmem,
        compiler_params=pltpu.CompilerParams(vmem_limit_bytes=16 * 1024 * 1024),
        name="gather",
    )(place, pairing, od, *parts)


def attention_kernel(chain, starts, joints, place_ref, pairing_ref, live_ref, qg_ref, *refs):
    held = refs[: len(starts) - 1]
    joint = refs[len(starts) - 1 : len(starts) - 1 + joints]
    od_ref, *parts, kv, acc = refs[len(starts) - 1 + joints :]
    pair = place_ref[0]
    half = place_ref[2]
    blocks = 2 * chain
    ctx = chain
    scale = 1.0 / math.sqrt(DIM)
    my_place = jnp.where(half == 0, pair, chain - 1 - pair)

    for ref, begin, end in zip(held, starts, starts[1:]):
        kv[begin:end, :] = ref[...]
    for ref, begin, end in zip(joint, starts[1:], starts[2:]):
        kv[begin:end, :] += ref[...]
    acc[...] = jnp.zeros_like(acc)

    keys_down = lax.broadcasted_iota(jnp.int32, (BLOCK, BLOCK), 0)
    rows_along = lax.broadcasted_iota(jnp.int32, (BLOCK, BLOCK), 1)
    lanes = lax.broadcasted_iota(jnp.int32, (1, blocks), 1)

    for b in range(2):
        holder = 2 * pair + b
        block = jnp.where(half == 0, holder, blocks - 1 - pairing_ref[holder])
        doc = qg_ref[b * BLOCK : b * BLOCK + PIECE, QG_WIDE:].astype(jnp.float32)
        doc = jnp.where(half == 0, doc[0:2], doc[2:4])
        begins = (doc[0:1] * BLOCK + doc[1:2]).astype(jnp.int32)
        live_row = live_ref[pl.ds(block, 1), :]
        slots = []
        bias = []
        for w in range(WINDOW):
            key_block = block - w
            mirrored = pairing_ref[jnp.clip(blocks - 1 - key_block, 0, ctx - 1)]
            held_by = jnp.where(key_block < ctx, key_block, mirrored)
            where_held = jnp.where(key_block < ctx, held_by // 2, chain - 1 - held_by // 2)
            away = my_place - where_held
            slot = jnp.where(away == 3, 6, jnp.where(away == -1, 7, 2 * away + held_by % 2))
            slot = jnp.where(key_block >= 0, jnp.clip(slot, 0, starts[-1] // BLOCK - 1), 0)
            slots.append(pl.multiple_of(slot * BLOCK, BLOCK))
            reach = begins - key_block * BLOCK
            if w == 0:
                seen = (keys_down >= reach) & (keys_down <= rows_along)
            else:
                listed = jnp.max(
                    jnp.where(lanes == key_block, live_row, 0), axis=1, keepdims=True
                )
                seen = keys_down >= jnp.where(listed == 1, reach, BLOCK)
            bias.append(jnp.where(seen, 0.0, NEGATIVE))
        bias = jnp.concatenate(bias, axis=0)
        bias = jnp.concatenate([bias, bias], axis=1)
        keys = jnp.concatenate([kv[pl.ds(s, BLOCK), :DIM] for s in slots], axis=0)
        values = jnp.concatenate([kv[pl.ds(s, BLOCK), DIM:] for s in slots], axis=0)
        rows = slice(b * BLOCK, (b + 1) * BLOCK)
        key_grad = None
        value_grad = None
        for h in range(0, GROUP, 2):
            first, second = h * DIM, (h + 1) * DIM
            shift = GROUP * DIM
            q = jnp.concatenate(
                [qg_ref[rows, first : first + DIM], qg_ref[rows, second : second + DIM]], axis=0
            )
            g = jnp.concatenate(
                [
                    qg_ref[rows, shift + first : shift + first + DIM],
                    qg_ref[rows, shift + second : shift + second + DIM],
                ],
                axis=0,
            )
            scores = dot(keys, q, 1, 1) + bias
            peak = jnp.max(scores, axis=0, keepdims=True)
            p = jnp.exp2((scores - peak) * (scale * math.log2(math.e)))
            p = p * (1.0 / jnp.sum(p, axis=0, keepdims=True))
            weights = p.astype(jnp.bfloat16)
            out = dot(values, weights, 0, 0)
            g_turned = g.astype(jnp.float32).T
            delta = jnp.sum(
                g_turned * out.astype(jnp.bfloat16).astype(jnp.float32), axis=0, keepdims=True
            )
            dweights = dot(values, g, 1, 1)
            dscores = (p * (dweights - delta)).astype(jnp.bfloat16)
            dq = dot(keys, dscores, 0, 0) * scale
            key_new = dot(dscores, q, 1, 0)
            value_new = dot(weights, g, 1, 0)
            key_grad = key_new if key_grad is None else key_grad + key_new
            value_grad = value_new if value_grad is None else value_grad + value_new
            out = out.T.astype(jnp.bfloat16)
            dq = dq.T.astype(jnp.bfloat16)
            od_ref[rows, first : first + DIM] = out[:BLOCK]
            od_ref[rows, second : second + DIM] = out[BLOCK:]
            od_ref[rows, shift + first : shift + first + DIM] = dq[:BLOCK]
            od_ref[rows, shift + second : shift + second + DIM] = dq[BLOCK:]
        key_grad = key_grad * scale
        for w, s in enumerate(slots):
            part = slice(w * BLOCK, (w + 1) * BLOCK)
            acc[pl.ds(s, BLOCK), :DIM] += key_grad[part]
            acc[pl.ds(s, BLOCK), DIM:] += value_grad[part]

    for ref, begin, end in zip(parts, starts, starts[1:]):
        ref[...] = acc[begin:end, :].astype(ref.dtype)


def attention(chain, place, pairing, live, qg, halo, joint):
    wide = 2 * DIM
    vmem = pl.BlockSpec(memory_space=pltpu.VMEM)
    smem = pl.BlockSpec(memory_space=pltpu.SMEM)
    starts = [0]
    for held in halo:
        starts.append(starts[-1] + held.shape[0])
    return pl.pallas_call(
        functools.partial(attention_kernel, chain, starts, len(joint)),
        out_shape=(
            jax.ShapeDtypeStruct((ROWS, QG_WIDE), jnp.bfloat16),
            jax.ShapeDtypeStruct((ROWS, wide), jnp.float32),
            *(jax.ShapeDtypeStruct(held.shape, jnp.bfloat16) for held in halo[1:]),
        ),
        in_specs=[smem, smem] + [vmem] * (2 + len(halo) + len(joint)),
        out_specs=(vmem,) * (1 + len(halo)),
        scratch_shapes=[
            pltpu.VMEM((starts[-1], wide), jnp.bfloat16),
            pltpu.VMEM((starts[-1], wide), jnp.float32),
        ],
        compiler_params=pltpu.CompilerParams(vmem_limit_bytes=32 * 1024 * 1024),
        cost_estimate=pl.CostEstimate(
            flops=2 * 5 * 2 * WINDOW * GROUP * BLOCK * BLOCK * DIM,
            bytes_accessed=3 * 1024 * 1024,
            transcendentals=2 * WINDOW * GROUP * BLOCK * BLOCK,
        ),
        name="attention",
    )(place, pairing, live, qg, *halo, *joint)


def body(pairing, doc_start, block_live, query, key, value, grad_out):
    pairs = lax.axis_size("pair")
    chain = 2 * pairs
    blocks = 2 * chain
    pair = lax.axis_index("pair")
    side = lax.axis_index("side")
    half = lax.axis_index("half")

    def linear(place):
        return place * 2 if place < pairs else (chain - 1 - place) * 2 + 1

    def steps(by, targets):
        return [(linear(s - by), linear(s)) for s in targets if 0 <= s - by < chain]

    early, late = range(pairs), range(pairs, chain)
    inner = [
        steps(by, early[: (by < 3) * pairs]) + steps(by, late[max(by, 0) :]) for by in (1, 2, 3)
    ]
    inner.append(steps(-1, late))
    outer = [steps(by, late[:by]) for by in (1, 2, 3)] + [[]]
    back = [[(b, a) for a, b in one + two] for one, two in zip(inner, outer)]

    def move(x, pairs_of):
        return lax.ppermute(x, ("pair", "half"), pairs_of)

    def exchange(x):
        return lax.all_to_all(x, ("side", "lane"), split_axis=0, concat_axis=0, tiled=True)

    place = jnp.stack([pair, side, half]).astype(jnp.int32)
    later = (half == 0) | (pairing[2 * pair + 1] < pairing[2 * pair])
    crossed = jnp.any(pairing[1 : chain - 1 : 2] == jnp.arange(2, chain, 2, dtype=jnp.int32))
    own = exchange(pack(key, value)).reshape(ROWS, 2 * DIM)
    split, later, crossed, place = lax.optimization_barrier(
        (pack(query, grad_out, doc_start.reshape(1, ROWS)), later, crossed, place)
    )
    split, own = lax.optimization_barrier((split, own))

    def finish(with_crossed, place, later, pairing, block_live, split, own):
        sent = [own, own]
        if with_crossed:
            sent += [jnp.where(later, own[BLOCK:], own[:BLOCK]), own[BLOCK:]]
        joint = [move(x, pairs_of) for x, pairs_of in zip(sent, outer) if pairs_of]
        split, joint = lax.optimization_barrier((split, joint))
        qg = exchange(split).reshape(ROWS, QG_WIDE + DIM)
        halo = [own] + [move(x, pairs_of) for x, pairs_of in zip(sent, inner)]
        od, own_grad, *partials = attention(chain, place, pairing, block_live, qg, halo, joint)
        order = sorted(range(len(partials)), key=[2, 1, 0, 3].__getitem__)
        moved = {i: move(partials[i], back[i]) for i in order}
        partials = [moved[i] for i in range(len(partials))]
        total = gather(place, pairing, od, (own_grad, *partials))
        return unpack(exchange(total.reshape(PARTS, PIECE, -1)))

    return lax.cond(
        crossed,
        functools.partial(finish, True),
        functools.partial(finish, False),
        place,
        later,
        pairing,
        block_live,
        split,
        own,
    )


def solution(mesh):
    ctx, head = mesh.devices.shape
    fine = Mesh(mesh.devices.reshape(ctx // 2, 2, 2, head // 2), ("pair", "side", "half", "lane"))
    tokens = P(("pair", "side", "half", "lane"), None)
    return jax.shard_map(
        body,
        mesh=fine,
        in_specs=(P(), P(("pair", "side")), P(), tokens, tokens, tokens, tokens),
        out_specs=(tokens,) * 4,
        check_vma=False,
    )
```

```python
import functools
import math

import jax
import jax.numpy as jnp
from jax import lax
from jax.experimental import pallas as pl
from jax.experimental.pallas import tpu as pltpu
from jax.sharding import Mesh
from jax.sharding import PartitionSpec as P

DIM = 128
BLOCK = 128
REACH = 4
WINDOW = REACH + 1
GROUP = 4
PARTS = 8
ROWS = 2 * BLOCK
PIECE = ROWS // PARTS
NEGATIVE = -1e30
QUERY_WIDE = GROUP * DIM
QG_WIDE = 2 * QUERY_WIDE


def dot(a, b, over_a, over_b):
    return lax.dot_general(
        a, b, (((over_a,), (over_b,)), ((), ())), preferred_element_type=jnp.float32
    )


def head_of(place, half):
    return (place + 2 * half) % PARTS


def pieces(whole, split, at, wide):
    if split.shape[0] == PARTS:
        half = lax.axis_index("half")
        heads = [head_of(p, half) for p in range(PARTS)]
    else:
        lanes = PARTS // 2
        heads = [
            head_of(side * lanes + lane, half)
            for side in range(2)
            for half in range(2)
            for lane in range(lanes)
        ]
    columns = [pl.multiple_of(head * wide, wide) for head in heads]
    return [
        (whole.at[:, pl.ds(column, wide)], split.at[p, :, pl.ds(at, wide)])
        for p, column in enumerate(columns)
    ]


def copies_of(first, second, split, at, wide, sems, cut):
    pairs = pieces(first, split, at, wide) + pieces(second, split, at + wide, wide)
    return [
        pltpu.make_async_copy(*((rows, piece) if cut else (piece, rows)), sems.at[i])
        for i, (rows, piece) in enumerate(pairs)
    ]


def pack_kernel(wide, first_ref, second_ref, *refs):
    if len(refs) == 2:
        out_ref, sems = refs
    else:
        doc_ref, out_ref, sems, doc_here, doc_sem = refs
        doc_copy = pltpu.make_async_copy(doc_ref, doc_here, doc_sem)
        doc_copy.start()
    copies = copies_of(first_ref, second_ref, out_ref, 0, wide, sems, True)
    for copy in copies:
        copy.start()
    if len(refs) > 2:
        doc_copy.wait()
        doc = doc_here[...]
        line = lax.broadcasted_iota(jnp.int32, (PIECE, BLOCK), 0)
        coded = jnp.where(line < 2, doc[:, :BLOCK], doc[:, BLOCK:])
        coded = jnp.where(line % 2 == 0, coded // BLOCK, coded % BLOCK)
        coded = coded.astype(jnp.float32).astype(jnp.bfloat16)
        for h in range(PARTS):
            out_ref[h, :, 2 * wide :] = coded
    for copy in copies:
        copy.wait()


def pack(first, second, parts, doc=None):
    hbm = pl.BlockSpec(memory_space=pltpu.HBM)
    wide = first.shape[1] // PARTS
    scratch = [pltpu.SemaphoreType.DMA((2 * parts,))]
    arrays = (first, second)
    sent = 2 * wide
    if doc is not None:
        scratch += [pltpu.VMEM((1, ROWS), jnp.int32), pltpu.SemaphoreType.DMA]
        arrays += (doc,)
        sent += DIM
    return pl.pallas_call(
        functools.partial(pack_kernel, wide),
        out_shape=jax.ShapeDtypeStruct((parts, PIECE, sent), jnp.bfloat16),
        in_specs=[hbm] * len(arrays),
        out_specs=pl.BlockSpec(memory_space=pltpu.VMEM),
        scratch_shapes=scratch,
        compiler_params=pltpu.CompilerParams(vmem_limit_bytes=(63 * 1024 + 256) * 1024),
        name="pack",
    )(*arrays)


def unpack_kernel(split_ref, att_ref, dq_ref, dk_ref, dv_ref, sems):
    copies = copies_of(att_ref, dq_ref, split_ref, 0, QUERY_WIDE, sems, False)
    copies += copies_of(dk_ref, dv_ref, split_ref, QG_WIDE, DIM, sems.at[2 * PARTS :], False)
    for copy in copies:
        copy.start()
    for copy in copies:
        copy.wait()


def unpack(split):
    hbm = pl.BlockSpec(memory_space=pltpu.HBM)
    wide = jax.ShapeDtypeStruct((PIECE, PARTS * QUERY_WIDE), jnp.bfloat16)
    narrow = jax.ShapeDtypeStruct((PIECE, PARTS * DIM), jnp.bfloat16)
    return pl.pallas_call(
        unpack_kernel,
        out_shape=(wide, wide, narrow, narrow),
        in_specs=[pl.BlockSpec(memory_space=pl.ANY)],
        out_specs=(hbm,) * 4,
        scratch_shapes=[pltpu.SemaphoreType.DMA((4 * PARTS,))],
        compiler_params=pltpu.CompilerParams(vmem_limit_bytes=16 * 1024 * 1024),
        name="unpack",
    )(split)


def gather_kernel(place_ref, pairing_ref, od_ref, own_ref, one_ref, two_ref, *refs):
    *extra, out_ref = refs
    out_ref[:, :QG_WIDE] = od_ref[...]
    total = own_ref[...] + one_ref[...].astype(jnp.float32) + two_ref[...].astype(jnp.float32)
    lower, upper = total[:BLOCK], total[BLOCK:]
    if extra:
        three_ref, back_ref = extra
        pair = place_ref[0]
        later = (place_ref[2] == 0) | (pairing_ref[2 * pair + 1] < pairing_ref[2 * pair])
        three = three_ref[...].astype(jnp.float32)
        lower = lower + jnp.where(later, 0.0, three)
        upper = upper + jnp.where(later, three, 0.0) + back_ref[...].astype(jnp.float32)
    out_ref[:BLOCK, QG_WIDE:] = lower.astype(jnp.bfloat16)
    out_ref[BLOCK:, QG_WIDE:] = upper.astype(jnp.bfloat16)


def gather(place, pairing, od, parts):
    vmem = pl.BlockSpec(memory_space=pltpu.VMEM)
    smem = pl.BlockSpec(memory_space=pltpu.SMEM)
    return pl.pallas_call(
        gather_kernel,
        out_shape=jax.ShapeDtypeStruct((ROWS, QG_WIDE + 2 * DIM), jnp.bfloat16),
        in_specs=[smem, smem] + [vmem] * (1 + len(parts)),
        out_specs=vmem,
        compiler_params=pltpu.CompilerParams(vmem_limit_bytes=16 * 1024 * 1024),
        name="gather",
    )(place, pairing, od, *parts)


def attention_kernel(chain, starts, joints, place_ref, pairing_ref, live_ref, qg_ref, *refs):
    held = refs[: len(starts) - 1]
    joint = refs[len(starts) - 1 : len(starts) - 1 + joints]
    od_ref, *parts, kv, acc = refs[len(starts) - 1 + joints :]
    pair = place_ref[0]
    half = place_ref[2]
    blocks = 2 * chain
    ctx = chain
    scale = 1.0 / math.sqrt(DIM)
    my_place = jnp.where(half == 0, pair, chain - 1 - pair)

    for ref, begin, end in zip(held, starts, starts[1:]):
        kv[begin:end, :] = ref[...]
    near_ref, *far = joint
    for ref, begin, end in zip(far, starts[2:], starts[3:]):
        kv[begin:end, :] += ref[...]

    @pl.when(my_place == chain // 2)
    def _():
        kv[starts[1] : starts[2], :] = near_ref[...]

    if len(starts) > 4:

        @pl.when(my_place == chain // 2 + 1)
        def _():
            kv[starts[3] : starts[4], :] = near_ref[BLOCK:, :]

    acc[...] = jnp.zeros_like(acc)

    keys_down = lax.broadcasted_iota(jnp.int32, (BLOCK, BLOCK), 0)
    rows_along = lax.broadcasted_iota(jnp.int32, (BLOCK, BLOCK), 1)
    lanes = lax.broadcasted_iota(jnp.int32, (1, blocks), 1)

    for b in range(2):
        holder = 2 * pair + b
        block = jnp.where(half == 0, holder, blocks - 1 - pairing_ref[holder])
        doc = qg_ref[b * BLOCK : b * BLOCK + PIECE, QG_WIDE:].astype(jnp.float32)
        doc = jnp.where(half == 0, doc[0:2], doc[2:4])
        begins = (doc[0:1] * BLOCK + doc[1:2]).astype(jnp.int32)
        live_row = live_ref[pl.ds(block, 1), :]
        slots = []
        bias = []
        for w in range(WINDOW):
            key_block = block - w
            mirrored = pairing_ref[jnp.clip(blocks - 1 - key_block, 0, ctx - 1)]
            held_by = jnp.where(key_block < ctx, key_block, mirrored)
            where_held = jnp.where(key_block < ctx, held_by // 2, chain - 1 - held_by // 2)
            away = my_place - where_held
            slot = jnp.where(away == 3, 6, jnp.where(away == -1, 7, 2 * away + held_by % 2))
            slot = jnp.where(key_block >= 0, jnp.clip(slot, 0, starts[-1] // BLOCK - 1), 0)
            slots.append(pl.multiple_of(slot * BLOCK, BLOCK))
            reach = begins - key_block * BLOCK
            if w == 0:
                seen = (keys_down >= reach) & (keys_down <= rows_along)
            else:
                listed = jnp.max(
                    jnp.where(lanes == key_block, live_row, 0), axis=1, keepdims=True
                )
                seen = keys_down >= jnp.where(listed == 1, reach, BLOCK)
            bias.append(jnp.where(seen, 0.0, NEGATIVE))
        bias = jnp.concatenate(bias, axis=0)
        bias = jnp.concatenate([bias, bias], axis=1)
        keys = jnp.concatenate([kv[pl.ds(s, BLOCK), :DIM] for s in slots], axis=0)
        values = jnp.concatenate([kv[pl.ds(s, BLOCK), DIM:] for s in slots], axis=0)
        rows = slice(b * BLOCK, (b + 1) * BLOCK)
        key_grad = None
        value_grad = None
        for h in range(0, GROUP, 2):
            first, second = h * DIM, (h + 1) * DIM
            shift = GROUP * DIM
            q = jnp.concatenate(
                [qg_ref[rows, first : first + DIM], qg_ref[rows, second : second + DIM]], axis=0
            )
            g = jnp.concatenate(
                [
                    qg_ref[rows, shift + first : shift + first + DIM],
                    qg_ref[rows, shift + second : shift + second + DIM],
                ],
                axis=0,
            )
            scores = dot(keys, q, 1, 1) + bias
            peak = jnp.max(scores, axis=0, keepdims=True)
            p = jnp.exp2((scores - peak) * (scale * math.log2(math.e)))
            p = p * (1.0 / jnp.sum(p, axis=0, keepdims=True))
            weights = p.astype(jnp.bfloat16)
            out = dot(values, weights, 0, 0)
            g_turned = g.astype(jnp.float32).T
            delta = jnp.sum(
                g_turned * out.astype(jnp.bfloat16).astype(jnp.float32), axis=0, keepdims=True
            )
            dweights = dot(values, g, 1, 1)
            dscores = (p * (dweights - delta)).astype(jnp.bfloat16)
            dq = dot(keys, dscores, 0, 0) * scale
            key_new = dot(dscores, q, 1, 0)
            value_new = dot(weights, g, 1, 0)
            key_grad = key_new if key_grad is None else key_grad + key_new
            value_grad = value_new if value_grad is None else value_grad + value_new
            out = out.T.astype(jnp.bfloat16)
            dq = dq.T.astype(jnp.bfloat16)
            od_ref[rows, first : first + DIM] = out[:BLOCK]
            od_ref[rows, second : second + DIM] = out[BLOCK:]
            od_ref[rows, shift + first : shift + first + DIM] = dq[:BLOCK]
            od_ref[rows, shift + second : shift + second + DIM] = dq[BLOCK:]
        key_grad = key_grad * scale
        for w, s in enumerate(slots):
            part = slice(w * BLOCK, (w + 1) * BLOCK)
            acc[pl.ds(s, BLOCK), :DIM] += key_grad[part]
            acc[pl.ds(s, BLOCK), DIM:] += value_grad[part]

    for ref, begin, end in zip(parts, starts, starts[1:]):
        ref[...] = acc[begin:end, :].astype(ref.dtype)


def attention(chain, place, pairing, live, qg, halo, joint):
    wide = 2 * DIM
    vmem = pl.BlockSpec(memory_space=pltpu.VMEM)
    smem = pl.BlockSpec(memory_space=pltpu.SMEM)
    starts = [0]
    for held in halo:
        starts.append(starts[-1] + held.shape[0])
    return pl.pallas_call(
        functools.partial(attention_kernel, chain, starts, len(joint)),
        out_shape=(
            jax.ShapeDtypeStruct((ROWS, QG_WIDE), jnp.bfloat16),
            jax.ShapeDtypeStruct((ROWS, wide), jnp.float32),
            *(jax.ShapeDtypeStruct(held.shape, jnp.bfloat16) for held in halo[1:]),
        ),
        in_specs=[smem, smem] + [vmem] * (2 + len(halo) + len(joint)),
        out_specs=(vmem,) * (1 + len(halo)),
        scratch_shapes=[
            pltpu.VMEM((starts[-1], wide), jnp.bfloat16),
            pltpu.VMEM((starts[-1], wide), jnp.float32),
        ],
        compiler_params=pltpu.CompilerParams(vmem_limit_bytes=32 * 1024 * 1024),
        cost_estimate=pl.CostEstimate(
            flops=2 * 5 * 2 * WINDOW * GROUP * BLOCK * BLOCK * DIM,
            bytes_accessed=3 * 1024 * 1024,
            transcendentals=2 * WINDOW * GROUP * BLOCK * BLOCK,
        ),
        name="attention",
    )(place, pairing, live, qg, *halo, *joint)


def body(pairing, doc_start, block_live, query, key, value, grad_out):
    pairs = lax.axis_size("pair")
    chain = 2 * pairs
    blocks = 2 * chain
    pair = lax.axis_index("pair")
    side = lax.axis_index("side")
    half = lax.axis_index("half")

    axes = ("pair", "side", "half", "lane")
    lanes = lax.axis_size("lane")

    def device(place, head):
        in_half = int(place >= pairs)
        in_pair = chain - 1 - place if in_half else place
        spot = next(p for p in range(PARTS) if head_of(p, in_half) == head)
        in_side, in_lane = divmod(spot, lanes)
        return ((in_pair * 2 + in_side) * 2 + in_half) * lanes + in_lane

    def steps(by, targets):
        return [
            (device(s - by, head), device(s, head))
            for s in targets
            if 0 <= s - by < chain
            for head in range(PARTS)
        ]

    early, late = range(pairs), range(pairs, chain)
    inner = [
        steps(by, early[: (by < 3) * pairs]) + steps(by, late[max(by, 0) :]) for by in (1, 2, 3)
    ]
    inner.append(steps(-1, late))
    outer = [steps(by, late[by == 3 : by]) for by in (1, 2, 3)] + [[]]
    relay = [steps(1, late[1:2]) + steps(-1, late[:1]), steps(2, late[2:3])]
    back = [[(b, a) for a, b in one + two] for one, two in zip(inner, outer)]

    def move(x, pairs_of):
        return lax.ppermute(x, axes, pairs_of)

    def exchange(x):
        return lax.all_to_all(x, ("side", "lane"), split_axis=0, concat_axis=0, tiled=True)

    place = jnp.stack([pair, side, half]).astype(jnp.int32)
    later = (half == 0) | (pairing[2 * pair + 1] < pairing[2 * pair])
    crossed = jnp.any(pairing[1 : chain - 1 : 2] == jnp.arange(2, chain, 2, dtype=jnp.int32))
    around = lax.all_to_all(
        pack(key, value, 2 * PARTS), ("side", "half", "lane"), split_axis=0, concat_axis=0, tiled=True
    ).reshape(2, 2, BLOCK, 2 * DIM)
    own = jnp.where(half == 0, around[:, 0], around[:, 1]).reshape(ROWS, 2 * DIM)
    near = jnp.where(half == 0, around[:, 1], around[:, 0]).reshape(ROWS, 2 * DIM)
    split, later, crossed, place = lax.optimization_barrier(
        (pack(query, grad_out, PARTS, doc_start.reshape(1, ROWS)), later, crossed, place)
    )
    split, own, near = lax.optimization_barrier((split, own, near))

    def finish(with_crossed, place, later, pairing, block_live, split, own, near):
        sent = [own, own]
        if with_crossed:
            sent += [jnp.where(later, own[BLOCK:], own[:BLOCK]), own[BLOCK:]]
        qg = exchange(split).reshape(ROWS, QG_WIDE + DIM)
        halo = [own] + [move(x, pairs_of) for x, pairs_of in zip(sent, inner)]
        joint = [near, move(near, relay[0])]
        if with_crossed:
            joint.append(move(near[BLOCK:], relay[1]))
        od, own_grad, *partials = attention(chain, place, pairing, block_live, qg, halo, joint)
        order = sorted(range(len(partials)), key=[2, 1, 0, 3].__getitem__)
        moved = {i: move(partials[i], back[i]) for i in order}
        partials = [moved[i] for i in range(len(partials))]
        total = gather(place, pairing, od, (own_grad, *partials))
        return unpack(exchange(total.reshape(PARTS, PIECE, -1)))

    return lax.cond(
        crossed,
        functools.partial(finish, True),
        functools.partial(finish, False),
        place,
        later,
        pairing,
        block_live,
        split,
        own,
        near,
    )


def solution(mesh):
    ctx, head = mesh.devices.shape
    fine = Mesh(mesh.devices.reshape(ctx // 2, 2, 2, head // 2), ("pair", "side", "half", "lane"))
    tokens = P(("pair", "side", "half", "lane"), None)
    return jax.shard_map(
        body,
        mesh=fine,
        in_specs=(P(), P(("pair", "side")), P(), tokens, tokens, tokens, tokens),
        out_specs=(tokens,) * 4,
        check_vma=False,
    )
```

```python
import functools
import math

import jax
import jax.numpy as jnp
from jax import lax
from jax.experimental import pallas as pl
from jax.experimental.pallas import tpu as pltpu
from jax.sharding import Mesh
from jax.sharding import PartitionSpec as P

DIM = 128
BLOCK = 128
REACH = 4
WINDOW = REACH + 1
GROUP = 4
PARTS = 8
ROWS = 2 * BLOCK
PIECE = ROWS // PARTS
NEGATIVE = -1e30
QUERY_WIDE = GROUP * DIM
QG_WIDE = 2 * QUERY_WIDE
WIDE = QG_WIDE + 2 * DIM


def dot(a, b, over_a, over_b):
    return lax.dot_general(
        a, b, (((over_a,), (over_b,)), ((), ())), preferred_element_type=jnp.float32
    )


def head_of(place, half):
    return (place + 2 * half) % PARTS


def pieces(whole, split, at, wide):
    half = lax.axis_index("half")
    columns = [pl.multiple_of(head_of(p, half) * wide, wide) for p in range(PARTS)]
    return [
        (whole.at[:, pl.ds(column, wide)], split.at[p, :, pl.ds(at, wide)])
        for p, column in enumerate(columns)
    ]


def copies_of(first, second, split, at, wide, sems, cut):
    pairs = pieces(first, split, at, wide) + pieces(second, split, at + wide, wide)
    return [
        pltpu.make_async_copy(*((rows, piece) if cut else (piece, rows)), sems.at[i])
        for i, (rows, piece) in enumerate(pairs)
    ]


def pack_kernel(doc_ref, q_ref, g_ref, k_ref, v_ref, out_ref, doc_here, sems, doc_sem):
    doc_copy = pltpu.make_async_copy(doc_ref, doc_here, doc_sem)
    doc_copy.start()
    copies = copies_of(q_ref, g_ref, out_ref, 0, QUERY_WIDE, sems, True)
    copies += copies_of(k_ref, v_ref, out_ref, QG_WIDE, DIM, sems.at[2 * PARTS :], True)
    for copy in copies:
        copy.start()
    doc_copy.wait()
    doc = doc_here[...]
    line = lax.broadcasted_iota(jnp.int32, (PIECE, BLOCK), 0)
    coded = jnp.where(line < 2, doc[:, :BLOCK], doc[:, BLOCK:])
    coded = jnp.where(line % 2 == 0, coded // BLOCK, coded % BLOCK)
    coded = coded.astype(jnp.float32).astype(jnp.bfloat16)
    for p in range(PARTS):
        out_ref[p, :, WIDE:] = coded
    for copy in copies:
        copy.wait()


def pack(doc, query, grad_out, key, value):
    hbm = pl.BlockSpec(memory_space=pltpu.HBM)
    return pl.pallas_call(
        pack_kernel,
        out_shape=jax.ShapeDtypeStruct((PARTS, PIECE, WIDE + DIM), jnp.bfloat16),
        in_specs=[hbm] * 5,
        out_specs=pl.BlockSpec(memory_space=pltpu.VMEM),
        scratch_shapes=[
            pltpu.VMEM((1, ROWS), jnp.int32),
            pltpu.SemaphoreType.DMA((4 * PARTS,)),
            pltpu.SemaphoreType.DMA,
        ],
        compiler_params=pltpu.CompilerParams(vmem_limit_bytes=(63 * 1024 + 256) * 1024),
        name="pack",
    )(doc, query, grad_out, key, value)


def unpack_kernel(split_ref, att_ref, dq_ref, dk_ref, dv_ref, sems):
    copies = copies_of(att_ref, dq_ref, split_ref, 0, QUERY_WIDE, sems, False)
    copies += copies_of(dk_ref, dv_ref, split_ref, QG_WIDE, DIM, sems.at[2 * PARTS :], False)
    for copy in copies:
        copy.start()
    for copy in copies:
        copy.wait()


def unpack(split):
    hbm = pl.BlockSpec(memory_space=pltpu.HBM)
    wide = jax.ShapeDtypeStruct((PIECE, PARTS * QUERY_WIDE), jnp.bfloat16)
    narrow = jax.ShapeDtypeStruct((PIECE, PARTS * DIM), jnp.bfloat16)
    return pl.pallas_call(
        unpack_kernel,
        out_shape=(wide, wide, narrow, narrow),
        in_specs=[pl.BlockSpec(memory_space=pl.ANY)],
        out_specs=(hbm,) * 4,
        scratch_shapes=[pltpu.SemaphoreType.DMA((4 * PARTS,))],
        compiler_params=pltpu.CompilerParams(vmem_limit_bytes=16 * 1024 * 1024),
        name="unpack",
    )(split)


def gather_kernel(place_ref, pairing_ref, od_ref, own_ref, one_ref, two_ref, *refs):
    *extra, out_ref = refs
    out_ref[:, :QG_WIDE] = od_ref[...]
    total = own_ref[...] + one_ref[...].astype(jnp.float32) + two_ref[...].astype(jnp.float32)
    lower, upper = total[:BLOCK], total[BLOCK:]
    if extra:
        three_ref, back_ref = extra
        pair = place_ref[0]
        later = (place_ref[2] == 0) | (pairing_ref[2 * pair + 1] < pairing_ref[2 * pair])
        three = three_ref[...].astype(jnp.float32)
        lower = lower + jnp.where(later, 0.0, three)
        upper = upper + jnp.where(later, three, 0.0) + back_ref[...].astype(jnp.float32)
    out_ref[:BLOCK, QG_WIDE:] = lower.astype(jnp.bfloat16)
    out_ref[BLOCK:, QG_WIDE:] = upper.astype(jnp.bfloat16)


def gather(place, pairing, od, parts):
    vmem = pl.BlockSpec(memory_space=pltpu.VMEM)
    smem = pl.BlockSpec(memory_space=pltpu.SMEM)
    return pl.pallas_call(
        gather_kernel,
        out_shape=jax.ShapeDtypeStruct((ROWS, QG_WIDE + 2 * DIM), jnp.bfloat16),
        in_specs=[smem, smem] + [vmem] * (1 + len(parts)),
        out_specs=vmem,
        compiler_params=pltpu.CompilerParams(vmem_limit_bytes=16 * 1024 * 1024),
        name="gather",
    )(place, pairing, od, *parts)


def attention_kernel(chain, starts, place_ref, pairing_ref, live_ref, qg_ref, *refs):
    held = refs[: len(starts) - 1]
    od_ref, *parts, kv, acc = refs[len(starts) - 1 :]
    pair = place_ref[0]
    half = place_ref[2]
    blocks = 2 * chain
    ctx = chain
    scale = 1.0 / math.sqrt(DIM)
    my_place = jnp.where(half == 0, pair, chain - 1 - pair)

    for ref, begin, end in zip(held, starts, starts[1:]):
        kv[begin:end, :] = ref[...]
    acc[...] = jnp.zeros_like(acc)

    keys_down = lax.broadcasted_iota(jnp.int32, (BLOCK, BLOCK), 0)
    rows_along = lax.broadcasted_iota(jnp.int32, (BLOCK, BLOCK), 1)
    lanes = lax.broadcasted_iota(jnp.int32, (1, blocks), 1)

    for b in range(2):
        holder = 2 * pair + b
        block = jnp.where(half == 0, holder, blocks - 1 - pairing_ref[holder])
        doc = qg_ref[b * BLOCK : b * BLOCK + PIECE, WIDE:].astype(jnp.float32)
        doc = jnp.where(half == 0, doc[0:2], doc[2:4])
        begins = (doc[0:1] * BLOCK + doc[1:2]).astype(jnp.int32)
        live_row = live_ref[pl.ds(block, 1), :]
        slots = []
        bias = []
        for w in range(WINDOW):
            key_block = block - w
            mirrored = pairing_ref[jnp.clip(blocks - 1 - key_block, 0, ctx - 1)]
            held_by = jnp.where(key_block < ctx, key_block, mirrored)
            where_held = jnp.where(key_block < ctx, held_by // 2, chain - 1 - held_by // 2)
            away = my_place - where_held
            slot = jnp.where(away == 3, 6, jnp.where(away == -1, 7, 2 * away + held_by % 2))
            slot = jnp.where(key_block >= 0, jnp.clip(slot, 0, starts[-1] // BLOCK - 1), 0)
            slots.append(pl.multiple_of(slot * BLOCK, BLOCK))
            reach = begins - key_block * BLOCK
            if w == 0:
                seen = (keys_down >= reach) & (keys_down <= rows_along)
            else:
                listed = jnp.max(
                    jnp.where(lanes == key_block, live_row, 0), axis=1, keepdims=True
                )
                seen = keys_down >= jnp.where(listed == 1, reach, BLOCK)
            bias.append(jnp.where(seen, 0.0, NEGATIVE))
        bias = jnp.concatenate(bias, axis=0)
        bias = jnp.concatenate([bias, bias], axis=1)
        keys = jnp.concatenate([kv[pl.ds(s, BLOCK), :DIM] for s in slots], axis=0)
        values = jnp.concatenate([kv[pl.ds(s, BLOCK), DIM:] for s in slots], axis=0)
        rows = slice(b * BLOCK, (b + 1) * BLOCK)
        key_grad = None
        value_grad = None
        for h in range(0, GROUP, 2):
            first, second = h * DIM, (h + 1) * DIM
            shift = GROUP * DIM
            q = jnp.concatenate(
                [qg_ref[rows, first : first + DIM], qg_ref[rows, second : second + DIM]], axis=0
            )
            g = jnp.concatenate(
                [
                    qg_ref[rows, shift + first : shift + first + DIM],
                    qg_ref[rows, shift + second : shift + second + DIM],
                ],
                axis=0,
            )
            scores = dot(keys, q, 1, 1) + bias
            peak = jnp.max(scores, axis=0, keepdims=True)
            p = jnp.exp2((scores - peak) * (scale * math.log2(math.e)))
            p = p * (1.0 / jnp.sum(p, axis=0, keepdims=True))
            weights = p.astype(jnp.bfloat16)
            out = dot(values, weights, 0, 0)
            g_turned = g.astype(jnp.float32).T
            delta = jnp.sum(
                g_turned * out.astype(jnp.bfloat16).astype(jnp.float32), axis=0, keepdims=True
            )
            dweights = dot(values, g, 1, 1)
            dscores = (p * (dweights - delta)).astype(jnp.bfloat16)
            dq = dot(keys, dscores, 0, 0) * scale
            key_new = dot(dscores, q, 1, 0)
            value_new = dot(weights, g, 1, 0)
            key_grad = key_new if key_grad is None else key_grad + key_new
            value_grad = value_new if value_grad is None else value_grad + value_new
            out = out.T.astype(jnp.bfloat16)
            dq = dq.T.astype(jnp.bfloat16)
            od_ref[rows, first : first + DIM] = out[:BLOCK]
            od_ref[rows, second : second + DIM] = out[BLOCK:]
            od_ref[rows, shift + first : shift + first + DIM] = dq[:BLOCK]
            od_ref[rows, shift + second : shift + second + DIM] = dq[BLOCK:]
        key_grad = key_grad * scale
        for w, s in enumerate(slots):
            part = slice(w * BLOCK, (w + 1) * BLOCK)
            acc[pl.ds(s, BLOCK), :DIM] += key_grad[part]
            acc[pl.ds(s, BLOCK), DIM:] += value_grad[part]

    for ref, begin, end in zip(parts, starts, starts[1:]):
        ref[...] = acc[begin:end, :].astype(ref.dtype)


def attention(chain, place, pairing, live, qg, halo):
    wide = 2 * DIM
    vmem = pl.BlockSpec(memory_space=pltpu.VMEM)
    smem = pl.BlockSpec(memory_space=pltpu.SMEM)
    starts = [0]
    for held in halo:
        starts.append(starts[-1] + held.shape[0])
    return pl.pallas_call(
        functools.partial(attention_kernel, chain, starts),
        out_shape=(
            jax.ShapeDtypeStruct((ROWS, QG_WIDE), jnp.bfloat16),
            jax.ShapeDtypeStruct((ROWS, wide), jnp.float32),
            *(jax.ShapeDtypeStruct(held.shape, jnp.bfloat16) for held in halo[1:]),
        ),
        in_specs=[smem, smem] + [vmem] * (2 + len(halo)),
        out_specs=(vmem,) * (1 + len(halo)),
        scratch_shapes=[
            pltpu.VMEM((starts[-1], wide), jnp.bfloat16),
            pltpu.VMEM((starts[-1], wide), jnp.float32),
        ],
        compiler_params=pltpu.CompilerParams(vmem_limit_bytes=32 * 1024 * 1024),
        cost_estimate=pl.CostEstimate(
            flops=2 * 5 * 2 * WINDOW * GROUP * BLOCK * BLOCK * DIM,
            bytes_accessed=3 * 1024 * 1024,
            transcendentals=2 * WINDOW * GROUP * BLOCK * BLOCK,
        ),
        name="attention",
    )(place, pairing, live, qg, *halo)


def body(pairing, doc_start, block_live, query, key, value, grad_out):
    pairs = lax.axis_size("pair")
    chain = 2 * pairs
    blocks = 2 * chain
    pair = lax.axis_index("pair")
    side = lax.axis_index("side")
    half = lax.axis_index("half")

    axes = ("pair", "side", "half", "lane")
    lanes = lax.axis_size("lane")

    def device(place, head):
        in_half = int(place >= pairs)
        in_pair = chain - 1 - place if in_half else place
        spot = next(p for p in range(PARTS) if head_of(p, in_half) == head)
        in_side, in_lane = divmod(spot, lanes)
        return ((in_pair * 2 + in_side) * 2 + in_half) * lanes + in_lane

    def steps(by, targets):
        return [
            (device(s - by, head), device(s, head))
            for s in targets
            if 0 <= s - by < chain
            for head in range(PARTS)
        ]

    forth = [
        steps(1, range(chain)),
        steps(2, range(chain)),
        steps(3, range(pairs + 1, chain)),
        steps(-1, range(pairs, chain)),
    ]
    back = [[(b, a) for a, b in pairs_of] for pairs_of in forth]

    def move(x, pairs_of):
        return lax.ppermute(x, axes, pairs_of)

    def exchange(x):
        return lax.all_to_all(x, ("side", "lane"), split_axis=0, concat_axis=0, tiled=True)

    place = jnp.stack([pair, side, half]).astype(jnp.int32)
    split = pack(doc_start.reshape(1, ROWS), query, grad_out, key, value)
    split, pairing = lax.optimization_barrier((split, pairing))
    later = (half == 0) | (pairing[2 * pair + 1] < pairing[2 * pair])
    crossed = jnp.any(pairing[1 : chain - 1 : 2] == jnp.arange(2, chain, 2, dtype=jnp.int32))
    arrived = exchange(split).reshape(ROWS, WIDE + DIM)

    def finish(with_crossed, place, later, pairing, block_live, arrived):
        own = arrived[:, QG_WIDE:WIDE]
        halo = [own, move(own, forth[0]), move(own, forth[1])]
        if with_crossed:
            halo.append(move(jnp.where(later, own[BLOCK:], own[:BLOCK]), forth[2]))
            halo.append(move(own[BLOCK:], forth[3]))
        od, own_grad, *partials = attention(chain, place, pairing, block_live, arrived, halo)
        partials = [move(part, pairs_of) for part, pairs_of in zip(partials, back)]
        total = gather(place, pairing, od, (own_grad, *partials))
        return unpack(exchange(total.reshape(PARTS, PIECE, -1)))

    return lax.cond(
        crossed,
        functools.partial(finish, True),
        functools.partial(finish, False),
        place,
        later,
        pairing,
        block_live,
        arrived,
    )


def solution(mesh):
    ctx, head = mesh.devices.shape
    fine = Mesh(mesh.devices.reshape(ctx // 2, 2, 2, head // 2), ("pair", "side", "half", "lane"))
    tokens = P(("pair", "side", "half", "lane"), None)
    return jax.shard_map(
        body,
        mesh=fine,
        in_specs=(P(), P(("pair", "side")), P(), tokens, tokens, tokens, tokens),
        out_specs=(tokens,) * 4,
        check_vma=False,
    )
```

```python
import functools
import math

import jax
import jax.numpy as jnp
from jax import lax
from jax.experimental import pallas as pl
from jax.experimental.pallas import tpu as pltpu
from jax.sharding import Mesh
from jax.sharding import PartitionSpec as P

DIM = 128
BLOCK = 128
REACH = 4
WINDOW = REACH + 1
GROUP = 4
PARTS = 8
ROWS = 2 * BLOCK
PIECE = ROWS // PARTS
NEGATIVE = -1e30
QUERY_WIDE = GROUP * DIM
QG_WIDE = 2 * QUERY_WIDE
WIDE = QG_WIDE + 2 * DIM


def dot(a, b, over_a, over_b):
    return lax.dot_general(
        a, b, (((over_a,), (over_b,)), ((), ())), preferred_element_type=jnp.float32
    )


def head_of(place, half):
    return (place + 2 * half) % PARTS


def spot(p):
    return p % 2 * (PARTS // 2) + p // 2


def rows_of(block, lane):
    first = (2 * lane + block) * PIECE
    return slice(first, first + PIECE)


def pieces(whole, split, at, wide):
    half = lax.axis_index("half")
    columns = [pl.multiple_of(head_of(spot(p), half) * wide, wide) for p in range(PARTS)]
    return [
        (whole.at[:, pl.ds(column, wide)], split.at[p, :, pl.ds(at, wide)])
        for p, column in enumerate(columns)
    ]


def copies_of(first, second, split, at, wide, sems, cut):
    pairs = pieces(first, split, at, wide) + pieces(second, split, at + wide, wide)
    return [
        pltpu.make_async_copy(*((rows, piece) if cut else (piece, rows)), sems.at[i])
        for i, (rows, piece) in enumerate(pairs)
    ]


def pack_kernel(doc_ref, q_ref, g_ref, k_ref, v_ref, out_ref, doc_here, sems, doc_sem):
    doc_copy = pltpu.make_async_copy(doc_ref, doc_here, doc_sem)
    doc_copy.start()
    copies = copies_of(q_ref, g_ref, out_ref, 0, QUERY_WIDE, sems, True)
    copies += copies_of(k_ref, v_ref, out_ref, QG_WIDE, DIM, sems.at[2 * PARTS :], True)
    for copy in copies:
        copy.start()
    doc_copy.wait()
    doc = doc_here[...]
    line = lax.broadcasted_iota(jnp.int32, (PIECE, BLOCK), 0)
    coded = jnp.where(line < 2, doc[:, :BLOCK], doc[:, BLOCK:])
    coded = jnp.where(line % 2 == 0, coded // BLOCK, coded % BLOCK)
    coded = coded.astype(jnp.float32).astype(jnp.bfloat16)
    for p in range(PARTS):
        out_ref[p, :, WIDE:] = coded
    for copy in copies:
        copy.wait()


def pack(doc, query, grad_out, key, value):
    hbm = pl.BlockSpec(memory_space=pltpu.HBM)
    return pl.pallas_call(
        pack_kernel,
        out_shape=jax.ShapeDtypeStruct((PARTS, PIECE, WIDE + DIM), jnp.bfloat16),
        in_specs=[hbm] * 5,
        out_specs=pl.BlockSpec(memory_space=pltpu.VMEM),
        scratch_shapes=[
            pltpu.VMEM((1, ROWS), jnp.int32),
            pltpu.SemaphoreType.DMA((4 * PARTS,)),
            pltpu.SemaphoreType.DMA,
        ],
        compiler_params=pltpu.CompilerParams(vmem_limit_bytes=(63 * 1024 + 256) * 1024),
        name="pack",
    )(doc, query, grad_out, key, value)


def unpack_kernel(split_ref, att_ref, dq_ref, dk_ref, dv_ref, sems):
    copies = copies_of(att_ref, dq_ref, split_ref, 0, QUERY_WIDE, sems, False)
    copies += copies_of(dk_ref, dv_ref, split_ref, QG_WIDE, DIM, sems.at[2 * PARTS :], False)
    for copy in copies:
        copy.start()
    for copy in copies:
        copy.wait()


def unpack(split):
    hbm = pl.BlockSpec(memory_space=pltpu.HBM)
    wide = jax.ShapeDtypeStruct((PIECE, PARTS * QUERY_WIDE), jnp.bfloat16)
    narrow = jax.ShapeDtypeStruct((PIECE, PARTS * DIM), jnp.bfloat16)
    return pl.pallas_call(
        unpack_kernel,
        out_shape=(wide, wide, narrow, narrow),
        in_specs=[pl.BlockSpec(memory_space=pl.ANY)],
        out_specs=(hbm,) * 4,
        scratch_shapes=[pltpu.SemaphoreType.DMA((4 * PARTS,))],
        compiler_params=pltpu.CompilerParams(vmem_limit_bytes=16 * 1024 * 1024),
        name="unpack",
    )(split)


def gather_kernel(place_ref, pairing_ref, od_ref, own_ref, one_ref, two_ref, *refs):
    *extra, out_ref = refs
    out_ref[:, :QG_WIDE] = od_ref[...]
    total = own_ref[...] + one_ref[...].astype(jnp.float32) + two_ref[...].astype(jnp.float32)
    lower, upper = total[:BLOCK], total[BLOCK:]
    if extra:
        three_ref, back_ref = extra
        pair = place_ref[0]
        later = (place_ref[2] == 0) | (pairing_ref[2 * pair + 1] < pairing_ref[2 * pair])
        three = three_ref[...].astype(jnp.float32)
        lower = lower + jnp.where(later, 0.0, three)
        upper = upper + jnp.where(later, three, 0.0) + back_ref[...].astype(jnp.float32)
    for b, part in enumerate((lower, upper)):
        part = part.astype(jnp.bfloat16)
        for lane in range(PARTS // 2):
            out_ref[rows_of(b, lane), QG_WIDE:] = part[lane * PIECE : (lane + 1) * PIECE]


def gather(place, pairing, od, parts):
    vmem = pl.BlockSpec(memory_space=pltpu.VMEM)
    smem = pl.BlockSpec(memory_space=pltpu.SMEM)
    return pl.pallas_call(
        gather_kernel,
        out_shape=jax.ShapeDtypeStruct((ROWS, QG_WIDE + 2 * DIM), jnp.bfloat16),
        in_specs=[smem, smem] + [vmem] * (1 + len(parts)),
        out_specs=vmem,
        compiler_params=pltpu.CompilerParams(vmem_limit_bytes=16 * 1024 * 1024),
        name="gather",
    )(place, pairing, od, *parts)


def attention_kernel(chain, starts, place_ref, pairing_ref, live_ref, qg_ref, *refs):
    held = refs[: len(starts) - 1]
    od_ref, *parts, kv, acc = refs[len(starts) - 1 :]
    pair = place_ref[0]
    half = place_ref[2]
    blocks = 2 * chain
    ctx = chain
    scale = 1.0 / math.sqrt(DIM)
    my_place = jnp.where(half == 0, pair, chain - 1 - pair)

    for ref, begin, end in zip(held, starts, starts[1:]):
        kv[begin:end, :] = ref[...]
    acc[...] = jnp.zeros_like(acc)

    keys_down = lax.broadcasted_iota(jnp.int32, (BLOCK, BLOCK), 0)
    rows_along = lax.broadcasted_iota(jnp.int32, (BLOCK, BLOCK), 1)
    lanes = lax.broadcasted_iota(jnp.int32, (1, blocks), 1)

    for b in range(2):
        holder = 2 * pair + b
        block = jnp.where(half == 0, holder, blocks - 1 - pairing_ref[holder])
        doc = qg_ref[rows_of(b, 0), WIDE:].astype(jnp.float32)
        doc = jnp.where(half == 0, doc[0:2], doc[2:4])
        begins = (doc[0:1] * BLOCK + doc[1:2]).astype(jnp.int32)
        live_row = live_ref[pl.ds(block, 1), :]
        slots = []
        bias = []
        for w in range(WINDOW):
            key_block = block - w
            mirrored = pairing_ref[jnp.clip(blocks - 1 - key_block, 0, ctx - 1)]
            held_by = jnp.where(key_block < ctx, key_block, mirrored)
            where_held = jnp.where(key_block < ctx, held_by // 2, chain - 1 - held_by // 2)
            away = my_place - where_held
            slot = jnp.where(away == 3, 6, jnp.where(away == -1, 7, 2 * away + held_by % 2))
            slot = jnp.where(key_block >= 0, jnp.clip(slot, 0, starts[-1] // BLOCK - 1), 0)
            slots.append(pl.multiple_of(slot * BLOCK, BLOCK))
            reach = begins - key_block * BLOCK
            if w == 0:
                seen = (keys_down >= reach) & (keys_down <= rows_along)
            else:
                listed = jnp.max(
                    jnp.where(lanes == key_block, live_row, 0), axis=1, keepdims=True
                )
                seen = keys_down >= jnp.where(listed == 1, reach, BLOCK)
            bias.append(jnp.where(seen, 0.0, NEGATIVE))
        bias = jnp.concatenate(bias, axis=0)
        bias = jnp.concatenate([bias, bias], axis=1)
        keys = jnp.concatenate([kv[pl.ds(s, BLOCK), :DIM] for s in slots], axis=0)
        values = jnp.concatenate([kv[pl.ds(s, BLOCK), DIM:] for s in slots], axis=0)
        lanes_of = [rows_of(b, lane) for lane in range(PARTS // 2)]
        key_grad = None
        value_grad = None
        for h in range(0, GROUP, 2):
            first, second = h * DIM, (h + 1) * DIM
            shift = GROUP * DIM
            columns = [slice(at, at + DIM) for at in (first, second)]
            g_columns = [slice(shift + at, shift + at + DIM) for at in (first, second)]
            q = jnp.concatenate([qg_ref[r, c] for c in columns for r in lanes_of], axis=0)
            g = jnp.concatenate([qg_ref[r, c] for c in g_columns for r in lanes_of], axis=0)
            scores = dot(keys, q, 1, 1) + bias
            peak = jnp.max(scores, axis=0, keepdims=True)
            p = jnp.exp2((scores - peak) * (scale * math.log2(math.e)))
            p = p * (1.0 / jnp.sum(p, axis=0, keepdims=True))
            weights = p.astype(jnp.bfloat16)
            out = dot(values, weights, 0, 0)
            g_turned = g.astype(jnp.float32).T
            delta = jnp.sum(
                g_turned * out.astype(jnp.bfloat16).astype(jnp.float32), axis=0, keepdims=True
            )
            dweights = dot(values, g, 1, 1)
            dscores = (p * (dweights - delta)).astype(jnp.bfloat16)
            dq = dot(keys, dscores, 0, 0) * scale
            key_new = dot(dscores, q, 1, 0)
            value_new = dot(weights, g, 1, 0)
            key_grad = key_new if key_grad is None else key_grad + key_new
            value_grad = value_new if value_grad is None else value_grad + value_new
            out = out.T.astype(jnp.bfloat16)
            dq = dq.T.astype(jnp.bfloat16)
            places = [(r, c, d) for c, d in zip(columns, g_columns) for r in lanes_of]
            for i, (r, c, d) in enumerate(places):
                od_ref[r, c] = out[i * PIECE : (i + 1) * PIECE]
                od_ref[r, d] = dq[i * PIECE : (i + 1) * PIECE]
        key_grad = key_grad * scale
        for w, s in enumerate(slots):
            part = slice(w * BLOCK, (w + 1) * BLOCK)
            acc[pl.ds(s, BLOCK), :DIM] += key_grad[part]
            acc[pl.ds(s, BLOCK), DIM:] += value_grad[part]

    for ref, begin, end in zip(parts, starts, starts[1:]):
        ref[...] = acc[begin:end, :].astype(ref.dtype)


def attention(chain, place, pairing, live, qg, halo):
    wide = 2 * DIM
    vmem = pl.BlockSpec(memory_space=pltpu.VMEM)
    smem = pl.BlockSpec(memory_space=pltpu.SMEM)
    starts = [0]
    for held in halo:
        starts.append(starts[-1] + held.shape[0])
    return pl.pallas_call(
        functools.partial(attention_kernel, chain, starts),
        out_shape=(
            jax.ShapeDtypeStruct((ROWS, QG_WIDE), jnp.bfloat16),
            jax.ShapeDtypeStruct((ROWS, wide), jnp.float32),
            *(jax.ShapeDtypeStruct(held.shape, jnp.bfloat16) for held in halo[1:]),
        ),
        in_specs=[smem, smem] + [vmem] * (2 + len(halo)),
        out_specs=(vmem,) * (1 + len(halo)),
        scratch_shapes=[
            pltpu.VMEM((starts[-1], wide), jnp.bfloat16),
            pltpu.VMEM((starts[-1], wide), jnp.float32),
        ],
        compiler_params=pltpu.CompilerParams(vmem_limit_bytes=32 * 1024 * 1024),
        cost_estimate=pl.CostEstimate(
            flops=2 * 5 * 2 * WINDOW * GROUP * BLOCK * BLOCK * DIM,
            bytes_accessed=3 * 1024 * 1024,
            transcendentals=2 * WINDOW * GROUP * BLOCK * BLOCK,
        ),
        name="attention",
    )(place, pairing, live, qg, *halo)


def body(pairing, doc_start, block_live, query, key, value, grad_out):
    pairs = lax.axis_size("pair")
    chain = 2 * pairs
    blocks = 2 * chain
    pair = lax.axis_index("pair")
    side = lax.axis_index("side")
    half = lax.axis_index("half")

    axes = ("pair", "side", "half", "lane")
    lanes = lax.axis_size("lane")

    def device(place, head):
        in_half = int(place >= pairs)
        in_pair = chain - 1 - place if in_half else place
        here = next(p for p in range(PARTS) if head_of(p, in_half) == head)
        in_side, in_lane = divmod(here, lanes)
        return ((in_pair * 2 + in_side) * 2 + in_half) * lanes + in_lane

    def steps(by, targets):
        return [
            (device(s - by, head), device(s, head))
            for s in targets
            if 0 <= s - by < chain
            for head in range(PARTS)
        ]

    forth = [
        steps(1, range(chain)),
        steps(2, range(chain)),
        steps(3, range(pairs + 1, chain)),
        steps(-1, range(pairs, chain)),
    ]
    back = [[(b, a) for a, b in pairs_of] for pairs_of in forth]

    def move(x, pairs_of):
        return lax.ppermute(x, axes, pairs_of)

    def exchange(x):
        order = [[spot(p) for p in range(PARTS)]]
        return lax.all_to_all(
            x, ("side", "lane"), split_axis=0, concat_axis=0, axis_index_groups=order, tiled=True
        )

    place = jnp.stack([pair, side, half]).astype(jnp.int32)
    split = pack(doc_start.reshape(1, ROWS), query, grad_out, key, value)
    split, pairing = lax.optimization_barrier((split, pairing))
    later = (half == 0) | (pairing[2 * pair + 1] < pairing[2 * pair])
    crossed = jnp.any(pairing[1 : chain - 1 : 2] == jnp.arange(2, chain, 2, dtype=jnp.int32))
    arrived = exchange(split).reshape(ROWS, WIDE + DIM)

    def finish(with_crossed, place, later, pairing, block_live, arrived):
        own = arrived[:, QG_WIDE:WIDE].reshape(lanes, 2, PIECE, 2 * DIM)
        own = own.transpose(1, 0, 2, 3).reshape(ROWS, 2 * DIM)
        halo = [own, move(own, forth[0]), move(own, forth[1])]
        if with_crossed:
            halo.append(move(jnp.where(later, own[BLOCK:], own[:BLOCK]), forth[2]))
            halo.append(move(own[BLOCK:], forth[3]))
        od, own_grad, *partials = attention(chain, place, pairing, block_live, arrived, halo)
        partials = [move(part, pairs_of) for part, pairs_of in zip(partials, back)]
        total = gather(place, pairing, od, (own_grad, *partials))
        return unpack(exchange(total.reshape(PARTS, PIECE, -1)))

    return lax.cond(
        crossed,
        functools.partial(finish, True),
        functools.partial(finish, False),
        place,
        later,
        pairing,
        block_live,
        arrived,
    )


def solution(mesh):
    ctx, head = mesh.devices.shape
    fine = Mesh(mesh.devices.reshape(ctx // 2, 2, 2, head // 2), ("pair", "side", "half", "lane"))
    tokens = P(("pair", "side", "half", "lane"), None)
    return jax.shard_map(
        body,
        mesh=fine,
        in_specs=(P(), P(("pair", "side")), P(), tokens, tokens, tokens, tokens),
        out_specs=(tokens,) * 4,
        check_vma=False,
    )
```

```python
import functools
import math

import jax
import jax.numpy as jnp
from jax import lax
from jax.experimental import pallas as pl
from jax.experimental.pallas import tpu as pltpu
from jax.sharding import Mesh
from jax.sharding import PartitionSpec as P

DIM = 128
BLOCK = 128
REACH = 4
WINDOW = REACH + 1
GROUP = 4
PARTS = 8
ROWS = 2 * BLOCK
PIECE = ROWS // PARTS
NEGATIVE = -1e30
QUERY_WIDE = GROUP * DIM
QG_WIDE = 2 * QUERY_WIDE
WIDE = QG_WIDE + 2 * DIM


def dot(a, b, over_a, over_b):
    return lax.dot_general(
        a, b, (((over_a,), (over_b,)), ((), ())), preferred_element_type=jnp.float32
    )


def head_of(place, half):
    return (place + 2 * half) % PARTS


def spot(p):
    return p % 2 * (PARTS // 2) + p // 2


def rows_of(block, lane):
    first = (2 * lane + block) * PIECE
    return slice(first, first + PIECE)


def pieces(whole, split, at, wide):
    half = lax.axis_index("half")
    columns = [pl.multiple_of(head_of(spot(p), half) * wide, wide) for p in range(PARTS)]
    return [
        (whole.at[:, pl.ds(column, wide)], split.at[p, :, pl.ds(at, wide)])
        for p, column in enumerate(columns)
    ]


def copies_of(first, second, split, at, wide, sems, cut):
    pairs = pieces(first, split, at, wide) + pieces(second, split, at + wide, wide)
    return [
        pltpu.make_async_copy(*((rows, piece) if cut else (piece, rows)), sems.at[i])
        for i, (rows, piece) in enumerate(pairs)
    ]


def pack_kernel(q_ref, g_ref, k_ref, v_ref, out_ref, sems):
    copies = copies_of(q_ref, g_ref, out_ref, 0, QUERY_WIDE, sems, True)
    copies += copies_of(k_ref, v_ref, out_ref, QG_WIDE, DIM, sems.at[2 * PARTS :], True)
    for copy in copies:
        copy.start()
    for copy in copies:
        copy.wait()


def pack(query, grad_out, key, value):
    hbm = pl.BlockSpec(memory_space=pltpu.HBM)
    return pl.pallas_call(
        pack_kernel,
        out_shape=jax.ShapeDtypeStruct((PARTS, PIECE, WIDE), jnp.bfloat16),
        in_specs=[hbm] * 4,
        out_specs=pl.BlockSpec(memory_space=pltpu.VMEM),
        scratch_shapes=[pltpu.SemaphoreType.DMA((4 * PARTS,))],
        compiler_params=pltpu.CompilerParams(vmem_limit_bytes=(63 * 1024 + 256) * 1024),
        name="pack",
    )(query, grad_out, key, value)


def unpack_kernel(split_ref, att_ref, dq_ref, dk_ref, dv_ref, sems):
    copies = copies_of(att_ref, dq_ref, split_ref, 0, QUERY_WIDE, sems, False)
    copies += copies_of(dk_ref, dv_ref, split_ref, QG_WIDE, DIM, sems.at[2 * PARTS :], False)
    for copy in copies:
        copy.start()
    for copy in copies:
        copy.wait()


def unpack(split):
    hbm = pl.BlockSpec(memory_space=pltpu.HBM)
    wide = jax.ShapeDtypeStruct((PIECE, PARTS * QUERY_WIDE), jnp.bfloat16)
    narrow = jax.ShapeDtypeStruct((PIECE, PARTS * DIM), jnp.bfloat16)
    return pl.pallas_call(
        unpack_kernel,
        out_shape=(wide, wide, narrow, narrow),
        in_specs=[pl.BlockSpec(memory_space=pl.ANY)],
        out_specs=(hbm,) * 4,
        scratch_shapes=[pltpu.SemaphoreType.DMA((4 * PARTS,))],
        compiler_params=pltpu.CompilerParams(vmem_limit_bytes=16 * 1024 * 1024),
        name="unpack",
    )(split)


def gather_kernel(place_ref, pairing_ref, od_ref, own_ref, one_ref, two_ref, *refs):
    *extra, out_ref = refs
    out_ref[:, :QG_WIDE] = od_ref[...]
    total = own_ref[...] + one_ref[...].astype(jnp.float32) + two_ref[...].astype(jnp.float32)
    lower, upper = total[:BLOCK], total[BLOCK:]
    if extra:
        three_ref, back_ref = extra
        pair = place_ref[0]
        later = (place_ref[2] == 0) | (pairing_ref[2 * pair + 1] < pairing_ref[2 * pair])
        three = three_ref[...].astype(jnp.float32)
        lower = lower + jnp.where(later, 0.0, three)
        upper = upper + jnp.where(later, three, 0.0) + back_ref[...].astype(jnp.float32)
    for b, part in enumerate((lower, upper)):
        part = part.astype(jnp.bfloat16)
        for lane in range(PARTS // 2):
            out_ref[rows_of(b, lane), QG_WIDE:] = part[lane * PIECE : (lane + 1) * PIECE]


def gather(place, pairing, od, parts):
    vmem = pl.BlockSpec(memory_space=pltpu.VMEM)
    smem = pl.BlockSpec(memory_space=pltpu.SMEM)
    return pl.pallas_call(
        gather_kernel,
        out_shape=jax.ShapeDtypeStruct((ROWS, QG_WIDE + 2 * DIM), jnp.bfloat16),
        in_specs=[smem, smem] + [vmem] * (1 + len(parts)),
        out_specs=vmem,
        compiler_params=pltpu.CompilerParams(vmem_limit_bytes=16 * 1024 * 1024),
        name="gather",
    )(place, pairing, od, *parts)


def attention_kernel(
    chain, starts, place_ref, pairing_ref, live_ref, doc_ref, doc_other_ref, qg_ref, *refs
):
    held = refs[: len(starts) - 1]
    od_ref, *parts, kv, acc = refs[len(starts) - 1 :]
    pair = place_ref[0]
    half = place_ref[2]
    blocks = 2 * chain
    ctx = chain
    scale = 1.0 / math.sqrt(DIM)
    my_place = jnp.where(half == 0, pair, chain - 1 - pair)

    for ref, begin, end in zip(held, starts, starts[1:]):
        kv[begin:end, :] = ref[...]
    acc[...] = jnp.zeros_like(acc)

    side = place_ref[1]
    mine = jnp.where(half == 0, doc_ref[:, :BLOCK], doc_ref[:, BLOCK:])
    other = jnp.where(half == 0, doc_other_ref[:, :BLOCK], doc_other_ref[:, BLOCK:])
    keys_down = lax.broadcasted_iota(jnp.int32, (BLOCK, BLOCK), 0)
    rows_along = lax.broadcasted_iota(jnp.int32, (BLOCK, BLOCK), 1)
    lanes = lax.broadcasted_iota(jnp.int32, (1, blocks), 1)

    for b in range(2):
        holder = 2 * pair + b
        block = jnp.where(half == 0, holder, blocks - 1 - pairing_ref[holder])
        begins = jnp.where(side == b, mine, other)
        live_row = live_ref[pl.ds(block, 1), :]
        slots = []
        bias = []
        for w in range(WINDOW):
            key_block = block - w
            mirrored = pairing_ref[jnp.clip(blocks - 1 - key_block, 0, ctx - 1)]
            held_by = jnp.where(key_block < ctx, key_block, mirrored)
            where_held = jnp.where(key_block < ctx, held_by // 2, chain - 1 - held_by // 2)
            away = my_place - where_held
            slot = jnp.where(away == 3, 6, jnp.where(away == -1, 7, 2 * away + held_by % 2))
            slot = jnp.where(key_block >= 0, jnp.clip(slot, 0, starts[-1] // BLOCK - 1), 0)
            slots.append(pl.multiple_of(slot * BLOCK, BLOCK))
            reach = begins - key_block * BLOCK
            if w == 0:
                seen = (keys_down >= reach) & (keys_down <= rows_along)
            else:
                listed = jnp.max(
                    jnp.where(lanes == key_block, live_row, 0), axis=1, keepdims=True
                )
                seen = keys_down >= jnp.where(listed == 1, reach, BLOCK)
            bias.append(jnp.where(seen, 0.0, NEGATIVE))
        bias = jnp.concatenate(bias, axis=0)
        bias = jnp.concatenate([bias, bias], axis=1)
        keys = jnp.concatenate([kv[pl.ds(s, BLOCK), :DIM] for s in slots], axis=0)
        values = jnp.concatenate([kv[pl.ds(s, BLOCK), DIM:] for s in slots], axis=0)
        lanes_of = [rows_of(b, lane) for lane in range(PARTS // 2)]
        key_grad = None
        value_grad = None
        for h in range(0, GROUP, 2):
            first, second = h * DIM, (h + 1) * DIM
            shift = GROUP * DIM
            columns = [slice(at, at + DIM) for at in (first, second)]
            g_columns = [slice(shift + at, shift + at + DIM) for at in (first, second)]
            q = jnp.concatenate([qg_ref[r, c] for c in columns for r in lanes_of], axis=0)
            g = jnp.concatenate([qg_ref[r, c] for c in g_columns for r in lanes_of], axis=0)
            scores = dot(keys, q, 1, 1) + bias
            peak = jnp.max(scores, axis=0, keepdims=True)
            p = jnp.exp2((scores - peak) * (scale * math.log2(math.e)))
            p = p * (1.0 / jnp.sum(p, axis=0, keepdims=True))
            weights = p.astype(jnp.bfloat16)
            out = dot(values, weights, 0, 0)
            g_turned = g.astype(jnp.float32).T
            delta = jnp.sum(
                g_turned * out.astype(jnp.bfloat16).astype(jnp.float32), axis=0, keepdims=True
            )
            dweights = dot(values, g, 1, 1)
            dscores = (p * (dweights - delta)).astype(jnp.bfloat16)
            dq = dot(keys, dscores, 0, 0) * scale
            key_new = dot(dscores, q, 1, 0)
            value_new = dot(weights, g, 1, 0)
            key_grad = key_new if key_grad is None else key_grad + key_new
            value_grad = value_new if value_grad is None else value_grad + value_new
            out = out.T.astype(jnp.bfloat16)
            dq = dq.T.astype(jnp.bfloat16)
            places = [(r, c, d) for c, d in zip(columns, g_columns) for r in lanes_of]
            for i, (r, c, d) in enumerate(places):
                od_ref[r, c] = out[i * PIECE : (i + 1) * PIECE]
                od_ref[r, d] = dq[i * PIECE : (i + 1) * PIECE]
        key_grad = key_grad * scale
        for w, s in enumerate(slots):
            part = slice(w * BLOCK, (w + 1) * BLOCK)
            acc[pl.ds(s, BLOCK), :DIM] += key_grad[part]
            acc[pl.ds(s, BLOCK), DIM:] += value_grad[part]

    for ref, begin, end in zip(parts, starts, starts[1:]):
        ref[...] = acc[begin:end, :].astype(ref.dtype)


def attention(chain, place, pairing, live, docs, qg, halo):
    wide = 2 * DIM
    vmem = pl.BlockSpec(memory_space=pltpu.VMEM)
    smem = pl.BlockSpec(memory_space=pltpu.SMEM)
    starts = [0]
    for held in halo:
        starts.append(starts[-1] + held.shape[0])
    return pl.pallas_call(
        functools.partial(attention_kernel, chain, starts),
        out_shape=(
            jax.ShapeDtypeStruct((ROWS, QG_WIDE), jnp.bfloat16),
            jax.ShapeDtypeStruct((ROWS, wide), jnp.float32),
            *(jax.ShapeDtypeStruct(held.shape, jnp.bfloat16) for held in halo[1:]),
        ),
        in_specs=[smem, smem] + [vmem] * (4 + len(halo)),
        out_specs=(vmem,) * (1 + len(halo)),
        scratch_shapes=[
            pltpu.VMEM((starts[-1], wide), jnp.bfloat16),
            pltpu.VMEM((starts[-1], wide), jnp.float32),
        ],
        compiler_params=pltpu.CompilerParams(vmem_limit_bytes=32 * 1024 * 1024),
        cost_estimate=pl.CostEstimate(
            flops=2 * 5 * 2 * WINDOW * GROUP * BLOCK * BLOCK * DIM,
            bytes_accessed=3 * 1024 * 1024,
            transcendentals=2 * WINDOW * GROUP * BLOCK * BLOCK,
        ),
        name="attention",
    )(place, pairing, live, *docs, qg, *halo)


def body(pairing, doc_start, block_live, query, key, value, grad_out):
    pairs = lax.axis_size("pair")
    chain = 2 * pairs
    blocks = 2 * chain
    pair = lax.axis_index("pair")
    side = lax.axis_index("side")
    half = lax.axis_index("half")

    axes = ("pair", "side", "half", "lane")
    lanes = lax.axis_size("lane")

    def device(place, head):
        in_half = int(place >= pairs)
        in_pair = chain - 1 - place if in_half else place
        here = next(p for p in range(PARTS) if head_of(p, in_half) == head)
        in_side, in_lane = divmod(here, lanes)
        return ((in_pair * 2 + in_side) * 2 + in_half) * lanes + in_lane

    def steps(by, targets):
        return [
            (device(s - by, head), device(s, head))
            for s in targets
            if 0 <= s - by < chain
            for head in range(PARTS)
        ]

    forth = [
        steps(1, range(chain)),
        steps(2, range(chain)),
        steps(3, range(pairs + 1, chain)),
        steps(-1, range(pairs, chain)),
    ]
    back = [[(b, a) for a, b in pairs_of] for pairs_of in forth]

    def move(x, pairs_of):
        return lax.ppermute(x, axes, pairs_of)

    def exchange(x):
        order = [[spot(p) for p in range(PARTS)]]
        return lax.all_to_all(
            x, ("side", "lane"), split_axis=0, concat_axis=0, axis_index_groups=order, tiled=True
        )

    place = jnp.stack([pair, side, half]).astype(jnp.int32)
    split = pack(query, grad_out, key, value)
    split, pairing, doc = lax.optimization_barrier((split, pairing, doc_start.reshape(1, ROWS)))
    doc_other = lax.ppermute(doc, "side", [(0, 1), (1, 0)])
    later = (half == 0) | (pairing[2 * pair + 1] < pairing[2 * pair])
    crossed = jnp.any(pairing[1 : chain - 1 : 2] == jnp.arange(2, chain, 2, dtype=jnp.int32))
    arrived = exchange(split).reshape(ROWS, WIDE)
    arrived, later, crossed, doc_other = lax.optimization_barrier(
        (arrived, later, crossed, doc_other)
    )

    def finish(with_crossed, place, later, pairing, block_live, doc, doc_other, arrived):
        own = arrived[:, QG_WIDE:WIDE].reshape(lanes, 2, PIECE, 2 * DIM)
        own = own.transpose(1, 0, 2, 3).reshape(ROWS, 2 * DIM)
        halo = [own, move(own, forth[0]), move(own, forth[1])]
        if with_crossed:
            halo.append(move(jnp.where(later, own[BLOCK:], own[:BLOCK]), forth[2]))
            halo.append(move(own[BLOCK:], forth[3]))
        od, own_grad, *partials = attention(
            chain, place, pairing, block_live, (doc, doc_other), arrived, halo
        )
        partials = [move(part, pairs_of) for part, pairs_of in zip(partials, back)]
        total = gather(place, pairing, od, (own_grad, *partials))
        return unpack(exchange(total.reshape(PARTS, PIECE, -1)))

    return lax.cond(
        crossed,
        functools.partial(finish, True),
        functools.partial(finish, False),
        place,
        later,
        pairing,
        block_live,
        doc,
        doc_other,
        arrived,
    )


def solution(mesh):
    ctx, head = mesh.devices.shape
    fine = Mesh(mesh.devices.reshape(ctx // 2, 2, 2, head // 2), ("pair", "side", "half", "lane"))
    tokens = P(("pair", "side", "half", "lane"), None)
    return jax.shard_map(
        body,
        mesh=fine,
        in_specs=(P(), P(("pair", "side")), P(), tokens, tokens, tokens, tokens),
        out_specs=(tokens,) * 4,
        check_vma=False,
    )
```

```python
import functools
import math

import jax
import jax.numpy as jnp
from jax import lax
from jax.experimental import pallas as pl
from jax.experimental.pallas import tpu as pltpu
from jax.sharding import Mesh
from jax.sharding import PartitionSpec as P

DIM = 128
BLOCK = 128
REACH = 4
WINDOW = REACH + 1
GROUP = 4
PARTS = 8
ROWS = 2 * BLOCK
PIECE = ROWS // PARTS
NEGATIVE = -1e30
QUERY_WIDE = GROUP * DIM
QG_WIDE = 2 * QUERY_WIDE
WIDE = QG_WIDE + 2 * DIM


def dot(a, b, over_a, over_b):
    return lax.dot_general(
        a, b, (((over_a,), (over_b,)), ((), ())), preferred_element_type=jnp.float32
    )


def head_of(place, half):
    return (place + 2 * half) % PARTS


def spot(p):
    return p % 2 * (PARTS // 2) + p // 2


def rows_of(block, lane):
    first = (2 * lane + block) * PIECE
    return slice(first, first + PIECE)


def pieces(whole, split, at, wide):
    half = lax.axis_index("half")
    columns = [pl.multiple_of(head_of(spot(p), half) * wide, wide) for p in range(PARTS)]
    return [
        (whole.at[:, pl.ds(column, wide)], split.at[p, :, pl.ds(at, wide)])
        for p, column in enumerate(columns)
    ]


def copies_of(first, second, split, at, wide, sems, cut):
    pairs = pieces(first, split, at, wide) + pieces(second, split, at + wide, wide)
    return [
        pltpu.make_async_copy(*((rows, piece) if cut else (piece, rows)), sems.at[i])
        for i, (rows, piece) in enumerate(pairs)
    ]


def pack_kernel(q_ref, g_ref, k_ref, v_ref, out_ref, sems):
    copies = copies_of(q_ref, g_ref, out_ref, 0, QUERY_WIDE, sems, True)
    copies += copies_of(k_ref, v_ref, out_ref, QG_WIDE, DIM, sems.at[2 * PARTS :], True)
    for copy in copies:
        copy.start()
    for copy in copies:
        copy.wait()


def pack(query, grad_out, key, value):
    hbm = pl.BlockSpec(memory_space=pltpu.HBM)
    return pl.pallas_call(
        pack_kernel,
        out_shape=jax.ShapeDtypeStruct((PARTS, PIECE, WIDE), jnp.bfloat16),
        in_specs=[hbm] * 4,
        out_specs=pl.BlockSpec(memory_space=pltpu.VMEM),
        scratch_shapes=[pltpu.SemaphoreType.DMA((4 * PARTS,))],
        compiler_params=pltpu.CompilerParams(vmem_limit_bytes=(63 * 1024 + 256) * 1024),
        name="pack",
    )(query, grad_out, key, value)


def unpack_kernel(split_ref, att_ref, dq_ref, dk_ref, dv_ref, sems):
    copies = copies_of(att_ref, dq_ref, split_ref, 0, QUERY_WIDE, sems, False)
    copies += copies_of(dk_ref, dv_ref, split_ref, QG_WIDE, DIM, sems.at[2 * PARTS :], False)
    for copy in copies:
        copy.start()
    for copy in copies:
        copy.wait()


def unpack(split):
    hbm = pl.BlockSpec(memory_space=pltpu.HBM)
    wide = jax.ShapeDtypeStruct((PIECE, PARTS * QUERY_WIDE), jnp.bfloat16)
    narrow = jax.ShapeDtypeStruct((PIECE, PARTS * DIM), jnp.bfloat16)
    return pl.pallas_call(
        unpack_kernel,
        out_shape=(wide, wide, narrow, narrow),
        in_specs=[pl.BlockSpec(memory_space=pl.ANY)],
        out_specs=(hbm,) * 4,
        scratch_shapes=[pltpu.SemaphoreType.DMA((4 * PARTS,))],
        compiler_params=pltpu.CompilerParams(vmem_limit_bytes=16 * 1024 * 1024),
        name="unpack",
    )(split)


def gather_kernel(place_ref, pairing_ref, od_ref, own_ref, one_ref, two_ref, *refs):
    *extra, out_ref = refs
    out_ref[:, :QG_WIDE] = od_ref[...]
    total = own_ref[...] + one_ref[...].astype(jnp.float32) + two_ref[...].astype(jnp.float32)
    lower, upper = total[:BLOCK], total[BLOCK:]
    if extra:
        three_ref, back_ref = extra
        pair = place_ref[0]
        later = (place_ref[2] == 0) | (pairing_ref[2 * pair + 1] < pairing_ref[2 * pair])
        three = three_ref[...].astype(jnp.float32)
        lower = lower + jnp.where(later, 0.0, three)
        upper = upper + jnp.where(later, three, 0.0) + back_ref[...].astype(jnp.float32)
    for b, part in enumerate((lower, upper)):
        part = part.astype(jnp.bfloat16)
        for lane in range(PARTS // 2):
            out_ref[rows_of(b, lane), QG_WIDE:] = part[lane * PIECE : (lane + 1) * PIECE]


def gather(place, pairing, od, parts):
    vmem = pl.BlockSpec(memory_space=pltpu.VMEM)
    smem = pl.BlockSpec(memory_space=pltpu.SMEM)
    return pl.pallas_call(
        gather_kernel,
        out_shape=jax.ShapeDtypeStruct((ROWS, QG_WIDE + 2 * DIM), jnp.bfloat16),
        in_specs=[smem, smem] + [vmem] * (1 + len(parts)),
        out_specs=vmem,
        compiler_params=pltpu.CompilerParams(vmem_limit_bytes=16 * 1024 * 1024),
        name="gather",
    )(place, pairing, od, *parts)


def output_order(count):
    return [0, 2, 1, 3, 4][:count]


def attention_kernel(
    chain, starts, place_ref, pairing_ref, live_ref, doc_ref, doc_other_ref, qg_ref, *refs
):
    held = refs[: len(starts) - 1]
    od_ref, *parts, kv, acc = refs[len(starts) - 1 :]
    pair = place_ref[0]
    half = place_ref[2]
    blocks = 2 * chain
    ctx = chain
    scale = 1.0 / math.sqrt(DIM)
    my_place = jnp.where(half == 0, pair, chain - 1 - pair)

    for ref, begin, end in zip(held, starts, starts[1:]):
        kv[begin:end, :] = ref[...]
    acc[...] = jnp.zeros_like(acc)

    side = place_ref[1]
    mine = jnp.where(half == 0, doc_ref[:, :BLOCK], doc_ref[:, BLOCK:])
    other = jnp.where(half == 0, doc_other_ref[:, :BLOCK], doc_other_ref[:, BLOCK:])
    keys_down = lax.broadcasted_iota(jnp.int32, (BLOCK, BLOCK), 0)
    rows_along = lax.broadcasted_iota(jnp.int32, (BLOCK, BLOCK), 1)
    lanes = lax.broadcasted_iota(jnp.int32, (1, blocks), 1)

    for b in range(2):
        holder = 2 * pair + b
        block = jnp.where(half == 0, holder, blocks - 1 - pairing_ref[holder])
        begins = jnp.where(side == b, mine, other)
        live_row = live_ref[pl.ds(block, 1), :]
        slots = []
        bias = []
        for w in range(WINDOW):
            key_block = block - w
            mirrored = pairing_ref[jnp.clip(blocks - 1 - key_block, 0, ctx - 1)]
            held_by = jnp.where(key_block < ctx, key_block, mirrored)
            where_held = jnp.where(key_block < ctx, held_by // 2, chain - 1 - held_by // 2)
            away = my_place - where_held
            slot = jnp.where(away == 3, 6, jnp.where(away == -1, 7, 2 * away + held_by % 2))
            slot = jnp.where(key_block >= 0, jnp.clip(slot, 0, starts[-1] // BLOCK - 1), 0)
            slots.append(pl.multiple_of(slot * BLOCK, BLOCK))
            reach = begins - key_block * BLOCK
            if w == 0:
                seen = (keys_down >= reach) & (keys_down <= rows_along)
            else:
                listed = jnp.max(
                    jnp.where(lanes == key_block, live_row, 0), axis=1, keepdims=True
                )
                seen = keys_down >= jnp.where(listed == 1, reach, BLOCK)
            bias.append(jnp.where(seen, 0.0, NEGATIVE))
        bias = jnp.concatenate(bias, axis=0)
        bias = jnp.concatenate([bias, bias], axis=1)
        keys = jnp.concatenate([kv[pl.ds(s, BLOCK), :DIM] for s in slots], axis=0)
        values = jnp.concatenate([kv[pl.ds(s, BLOCK), DIM:] for s in slots], axis=0)
        keys_turned = keys.T
        values_turned = values.T
        lanes_of = [rows_of(b, lane) for lane in range(PARTS // 2)]
        key_grad = None
        value_grad = None
        for h in range(0, GROUP, 2):
            first, second = h * DIM, (h + 1) * DIM
            shift = GROUP * DIM
            columns = [slice(at, at + DIM) for at in (first, second)]
            g_columns = [slice(shift + at, shift + at + DIM) for at in (first, second)]
            q = jnp.concatenate([qg_ref[r, c] for c in columns for r in lanes_of], axis=0)
            g = jnp.concatenate([qg_ref[r, c] for c in g_columns for r in lanes_of], axis=0)
            scores = dot(keys, q, 1, 1) + bias
            peak = jnp.max(scores, axis=0, keepdims=True)
            p = jnp.exp2((scores - peak) * (scale * math.log2(math.e)))
            p = p * (1.0 / jnp.sum(p, axis=0, keepdims=True))
            weights = p.astype(jnp.bfloat16)
            out = dot(values_turned, weights, 1, 0)
            g_turned = g.astype(jnp.float32).T
            delta = jnp.sum(
                g_turned * out.astype(jnp.bfloat16).astype(jnp.float32), axis=0, keepdims=True
            )
            dweights = dot(values, g, 1, 1)
            dscores = (p * (dweights - delta)).astype(jnp.bfloat16)
            dq = dot(keys_turned, dscores, 1, 0) * scale
            key_new = dot(dscores, q, 1, 0)
            value_new = dot(weights, g, 1, 0)
            key_grad = key_new if key_grad is None else key_grad + key_new
            value_grad = value_new if value_grad is None else value_grad + value_new
            out = out.T.astype(jnp.bfloat16)
            dq = dq.T.astype(jnp.bfloat16)
            places = [(r, c, d) for c, d in zip(columns, g_columns) for r in lanes_of]
            for i, (r, c, d) in enumerate(places):
                od_ref[r, c] = out[i * PIECE : (i + 1) * PIECE]
                od_ref[r, d] = dq[i * PIECE : (i + 1) * PIECE]
        key_grad = key_grad * scale
        for w, s in enumerate(slots):
            part = slice(w * BLOCK, (w + 1) * BLOCK)
            acc[pl.ds(s, BLOCK), :DIM] += key_grad[part]
            acc[pl.ds(s, BLOCK), DIM:] += value_grad[part]

    for ref, i in zip(parts, output_order(len(parts))):
        ref[...] = acc[starts[i] : starts[i + 1], :].astype(ref.dtype)


def attention(chain, place, pairing, live, docs, qg, halo):
    wide = 2 * DIM
    vmem = pl.BlockSpec(memory_space=pltpu.VMEM)
    smem = pl.BlockSpec(memory_space=pltpu.SMEM)
    starts = [0]
    for held in halo:
        starts.append(starts[-1] + held.shape[0])
    return pl.pallas_call(
        functools.partial(attention_kernel, chain, starts),
        out_shape=(
            jax.ShapeDtypeStruct((ROWS, QG_WIDE), jnp.bfloat16),
            jax.ShapeDtypeStruct((ROWS, wide), jnp.float32),
            *(
                jax.ShapeDtypeStruct(halo[i].shape, jnp.bfloat16)
                for i in output_order(len(halo))[1:]
            ),
        ),
        in_specs=[smem, smem] + [vmem] * (4 + len(halo)),
        out_specs=(vmem,) * (1 + len(halo)),
        scratch_shapes=[
            pltpu.VMEM((starts[-1], wide), jnp.bfloat16),
            pltpu.VMEM((starts[-1], wide), jnp.float32),
        ],
        compiler_params=pltpu.CompilerParams(vmem_limit_bytes=32 * 1024 * 1024),
        cost_estimate=pl.CostEstimate(
            flops=2 * 5 * 2 * WINDOW * GROUP * BLOCK * BLOCK * DIM,
            bytes_accessed=3 * 1024 * 1024,
            transcendentals=2 * WINDOW * GROUP * BLOCK * BLOCK,
        ),
        name="attention",
    )(place, pairing, live, *docs, qg, *halo)


def body(pairing, doc_start, block_live, query, key, value, grad_out):
    pairs = lax.axis_size("pair")
    chain = 2 * pairs
    blocks = 2 * chain
    pair = lax.axis_index("pair")
    side = lax.axis_index("side")
    half = lax.axis_index("half")

    axes = ("pair", "side", "half", "lane")
    lanes = lax.axis_size("lane")

    def device(place, head):
        in_half = int(place >= pairs)
        in_pair = chain - 1 - place if in_half else place
        here = next(p for p in range(PARTS) if head_of(p, in_half) == head)
        in_side, in_lane = divmod(here, lanes)
        return ((in_pair * 2 + in_side) * 2 + in_half) * lanes + in_lane

    def steps(by, targets):
        return [
            (device(s - by, head), device(s, head))
            for s in targets
            if 0 <= s - by < chain
            for head in range(PARTS)
        ]

    forth = [
        steps(1, range(chain)),
        steps(2, range(chain)),
        steps(3, range(pairs + 1, chain)),
        steps(-1, range(pairs, chain)),
    ]
    back = [[(b, a) for a, b in pairs_of] for pairs_of in forth]

    def move(x, pairs_of):
        return lax.ppermute(x, axes, pairs_of)

    def exchange(x):
        order = [[spot(p) for p in range(PARTS)]]
        return lax.all_to_all(
            x, ("side", "lane"), split_axis=0, concat_axis=0, axis_index_groups=order, tiled=True
        )

    place = jnp.stack([pair, side, half]).astype(jnp.int32)
    split = pack(query, grad_out, key, value)
    split, pairing, doc = lax.optimization_barrier((split, pairing, doc_start.reshape(1, ROWS)))
    doc_other = lax.ppermute(doc, "side", [(0, 1), (1, 0)])
    later = (half == 0) | (pairing[2 * pair + 1] < pairing[2 * pair])
    crossed = jnp.any(pairing[1 : chain - 1 : 2] == jnp.arange(2, chain, 2, dtype=jnp.int32))
    arrived = exchange(split).reshape(ROWS, WIDE)
    arrived, later, crossed, doc_other = lax.optimization_barrier(
        (arrived, later, crossed, doc_other)
    )

    def finish(with_crossed, place, later, pairing, block_live, doc, doc_other, arrived):
        own = arrived[:, QG_WIDE:WIDE].reshape(lanes, 2, PIECE, 2 * DIM)
        own = own.transpose(1, 0, 2, 3).reshape(ROWS, 2 * DIM)
        halo = [own, move(own, forth[0]), move(own, forth[1])]
        if with_crossed:
            halo.append(move(jnp.where(later, own[BLOCK:], own[:BLOCK]), forth[2]))
            halo.append(move(own[BLOCK:], forth[3]))
        od, *partials = attention(
            chain, place, pairing, block_live, (doc, doc_other), arrived, halo
        )
        moved = {}
        for i, part in zip(output_order(len(partials)), partials):
            moved[i] = move(part, back[i - 1]) if i else part
        total = gather(place, pairing, od, [moved[i] for i in range(len(moved))])
        return unpack(exchange(total.reshape(PARTS, PIECE, -1)))

    return lax.cond(
        crossed,
        functools.partial(finish, True),
        functools.partial(finish, False),
        place,
        later,
        pairing,
        block_live,
        doc,
        doc_other,
        arrived,
    )


def solution(mesh):
    ctx, head = mesh.devices.shape
    fine = Mesh(mesh.devices.reshape(ctx // 2, 2, 2, head // 2), ("pair", "side", "half", "lane"))
    tokens = P(("pair", "side", "half", "lane"), None)
    return jax.shard_map(
        body,
        mesh=fine,
        in_specs=(P(), P(("pair", "side")), P(), tokens, tokens, tokens, tokens),
        out_specs=(tokens,) * 4,
        check_vma=False,
    )
```

```python
import functools
import math

import jax
import jax.numpy as jnp
from jax import lax
from jax.experimental import pallas as pl
from jax.experimental.pallas import tpu as pltpu
from jax.sharding import Mesh
from jax.sharding import PartitionSpec as P

DIM = 128
BLOCK = 128
REACH = 4
WINDOW = REACH + 1
GROUP = 4
PARTS = 8
ROWS = 2 * BLOCK
PIECE = ROWS // PARTS
NEGATIVE = -1e30
QUERY_WIDE = GROUP * DIM
QG_WIDE = 2 * QUERY_WIDE
WIDE = QG_WIDE + 2 * DIM


def dot(a, b, over_a, over_b):
    return lax.dot_general(
        a, b, (((over_a,), (over_b,)), ((), ())), preferred_element_type=jnp.float32
    )


def head_of(place, half):
    return (place + 2 * half) % PARTS


def spot(p):
    return p % 2 * (PARTS // 2) + p // 2


def rows_of(block, lane):
    first = (2 * lane + block) * PIECE
    return slice(first, first + PIECE)


def pieces(whole, split, at, wide):
    half = lax.axis_index("half")
    columns = [pl.multiple_of(head_of(spot(p), half) * wide, wide) for p in range(PARTS)]
    return [
        (whole.at[:, pl.ds(column, wide)], split.at[p, :, pl.ds(at, wide)])
        for p, column in enumerate(columns)
    ]


def copies_of(first, second, split, at, wide, sems, cut):
    pairs = pieces(first, split, at, wide) + pieces(second, split, at + wide, wide)
    return [
        pltpu.make_async_copy(*((rows, piece) if cut else (piece, rows)), sems.at[i])
        for i, (rows, piece) in enumerate(pairs)
    ]


def pack_kernel(q_ref, g_ref, k_ref, v_ref, out_ref, sems):
    copies = copies_of(q_ref, g_ref, out_ref, 0, QUERY_WIDE, sems, True)
    copies += copies_of(k_ref, v_ref, out_ref, QG_WIDE, DIM, sems.at[2 * PARTS :], True)
    for copy in copies:
        copy.start()
    for copy in copies:
        copy.wait()


def pack(query, grad_out, key, value):
    hbm = pl.BlockSpec(memory_space=pltpu.HBM)
    return pl.pallas_call(
        pack_kernel,
        out_shape=jax.ShapeDtypeStruct((PARTS, PIECE, WIDE), jnp.bfloat16),
        in_specs=[hbm] * 4,
        out_specs=pl.BlockSpec(memory_space=pltpu.VMEM),
        scratch_shapes=[pltpu.SemaphoreType.DMA((4 * PARTS,))],
        compiler_params=pltpu.CompilerParams(vmem_limit_bytes=(63 * 1024 + 256) * 1024),
        name="pack",
    )(query, grad_out, key, value)


def unpack_kernel(split_ref, att_ref, dq_ref, dk_ref, dv_ref, sems):
    copies = copies_of(att_ref, dq_ref, split_ref, 0, QUERY_WIDE, sems, False)
    copies += copies_of(dk_ref, dv_ref, split_ref, QG_WIDE, DIM, sems.at[2 * PARTS :], False)
    for copy in copies:
        copy.start()
    for copy in copies:
        copy.wait()


def unpack(split):
    hbm = pl.BlockSpec(memory_space=pltpu.HBM)
    wide = jax.ShapeDtypeStruct((PIECE, PARTS * QUERY_WIDE), jnp.bfloat16)
    narrow = jax.ShapeDtypeStruct((PIECE, PARTS * DIM), jnp.bfloat16)
    return pl.pallas_call(
        unpack_kernel,
        out_shape=(wide, wide, narrow, narrow),
        in_specs=[pl.BlockSpec(memory_space=pl.ANY)],
        out_specs=(hbm,) * 4,
        scratch_shapes=[pltpu.SemaphoreType.DMA((4 * PARTS,))],
        compiler_params=pltpu.CompilerParams(vmem_limit_bytes=16 * 1024 * 1024),
        name="unpack",
    )(split)


def gather_kernel(place_ref, pairing_ref, att_ref, dq_ref, own_ref, one_ref, two_ref, *refs):
    *extra, out_ref = refs
    out_ref[:, :QUERY_WIDE] = att_ref[...]
    out_ref[:, QUERY_WIDE:QG_WIDE] = dq_ref[...]
    total = own_ref[...] + one_ref[...].astype(jnp.float32) + two_ref[...].astype(jnp.float32)
    lower, upper = total[:BLOCK], total[BLOCK:]
    if extra:
        three_ref, back_ref = extra
        pair = place_ref[0]
        later = (place_ref[2] == 0) | (pairing_ref[2 * pair + 1] < pairing_ref[2 * pair])
        three = three_ref[...].astype(jnp.float32)
        lower = lower + jnp.where(later, 0.0, three)
        upper = upper + jnp.where(later, three, 0.0) + back_ref[...].astype(jnp.float32)
    for b, part in enumerate((lower, upper)):
        part = part.astype(jnp.bfloat16)
        for lane in range(PARTS // 2):
            out_ref[rows_of(b, lane), QG_WIDE:] = part[lane * PIECE : (lane + 1) * PIECE]


def gather(place, pairing, att, dq, parts):
    vmem = pl.BlockSpec(memory_space=pltpu.VMEM)
    smem = pl.BlockSpec(memory_space=pltpu.SMEM)
    return pl.pallas_call(
        gather_kernel,
        out_shape=jax.ShapeDtypeStruct((ROWS, QG_WIDE + 2 * DIM), jnp.bfloat16),
        in_specs=[smem, smem] + [vmem] * (2 + len(parts)),
        out_specs=vmem,
        compiler_params=pltpu.CompilerParams(vmem_limit_bytes=16 * 1024 * 1024),
        name="gather",
    )(place, pairing, att, dq, *parts)


def output_order(count):
    return [0, 2, 1, 3, 4][:count]


def attention_kernel(
    chain, starts, place_ref, pairing_ref, live_ref, doc_ref, doc_other_ref, qg_ref, *refs
):
    held = refs[: len(starts) - 1]
    od_ref, ds_ref, kt_ref, *parts, kv, acc = refs[len(starts) - 1 :]
    pair = place_ref[0]
    half = place_ref[2]
    blocks = 2 * chain
    ctx = chain
    scale = 1.0 / math.sqrt(DIM)
    my_place = jnp.where(half == 0, pair, chain - 1 - pair)

    for ref, begin, end in zip(held, starts, starts[1:]):
        kv[begin:end, :] = ref[...]
    acc[...] = jnp.zeros_like(acc)

    side = place_ref[1]
    mine = jnp.where(half == 0, doc_ref[:, :BLOCK], doc_ref[:, BLOCK:])
    other = jnp.where(half == 0, doc_other_ref[:, :BLOCK], doc_other_ref[:, BLOCK:])
    keys_down = lax.broadcasted_iota(jnp.int32, (BLOCK, BLOCK), 0)
    rows_along = lax.broadcasted_iota(jnp.int32, (BLOCK, BLOCK), 1)
    lanes = lax.broadcasted_iota(jnp.int32, (1, blocks), 1)

    for b in range(2):
        holder = 2 * pair + b
        block = jnp.where(half == 0, holder, blocks - 1 - pairing_ref[holder])
        begins = jnp.where(side == b, mine, other)
        live_row = live_ref[pl.ds(block, 1), :]
        slots = []
        bias = []
        for w in range(WINDOW):
            key_block = block - w
            mirrored = pairing_ref[jnp.clip(blocks - 1 - key_block, 0, ctx - 1)]
            held_by = jnp.where(key_block < ctx, key_block, mirrored)
            where_held = jnp.where(key_block < ctx, held_by // 2, chain - 1 - held_by // 2)
            away = my_place - where_held
            slot = jnp.where(away == 3, 6, jnp.where(away == -1, 7, 2 * away + held_by % 2))
            slot = jnp.where(key_block >= 0, jnp.clip(slot, 0, starts[-1] // BLOCK - 1), 0)
            slots.append(pl.multiple_of(slot * BLOCK, BLOCK))
            reach = begins - key_block * BLOCK
            if w == 0:
                seen = (keys_down >= reach) & (keys_down <= rows_along)
            else:
                listed = jnp.max(
                    jnp.where(lanes == key_block, live_row, 0), axis=1, keepdims=True
                )
                seen = keys_down >= jnp.where(listed == 1, reach, BLOCK)
            bias.append(jnp.where(seen, 0.0, NEGATIVE))
        bias = jnp.concatenate(bias, axis=0)
        bias = jnp.concatenate([bias, bias], axis=1)
        keys = jnp.concatenate([kv[pl.ds(s, BLOCK), :DIM] for s in slots], axis=0)
        values = jnp.concatenate([kv[pl.ds(s, BLOCK), DIM:] for s in slots], axis=0)
        keys_turned = keys.T
        values_turned = values.T
        kt_ref[b] = keys_turned
        lanes_of = [rows_of(b, lane) for lane in range(PARTS // 2)]
        key_grad = None
        value_grad = None
        for h in range(0, GROUP, 2):
            first, second = h * DIM, (h + 1) * DIM
            shift = GROUP * DIM
            columns = [slice(at, at + DIM) for at in (first, second)]
            g_columns = [slice(shift + at, shift + at + DIM) for at in (first, second)]
            q = jnp.concatenate([qg_ref[r, c] for c in columns for r in lanes_of], axis=0)
            g = jnp.concatenate([qg_ref[r, c] for c in g_columns for r in lanes_of], axis=0)
            scores = dot(keys, q, 1, 1) + bias
            peak = jnp.max(scores, axis=0, keepdims=True)
            p = jnp.exp2((scores - peak) * (scale * math.log2(math.e)))
            p = p * (1.0 / jnp.sum(p, axis=0, keepdims=True))
            weights = p.astype(jnp.bfloat16)
            out = dot(values_turned, weights, 1, 0)
            g_turned = g.astype(jnp.float32).T
            delta = jnp.sum(
                g_turned * out.astype(jnp.bfloat16).astype(jnp.float32), axis=0, keepdims=True
            )
            dweights = dot(values, g, 1, 1)
            dscores = (p * (dweights - delta)).astype(jnp.bfloat16)
            ds_ref[b, h // 2] = dscores
            key_new = dot(dscores, q, 1, 0)
            value_new = dot(weights, g, 1, 0)
            key_grad = key_new if key_grad is None else key_grad + key_new
            value_grad = value_new if value_grad is None else value_grad + value_new
            out = out.T.astype(jnp.bfloat16)
            for i, (r, c) in enumerate((r, c) for c in columns for r in lanes_of):
                od_ref[r, c] = out[i * PIECE : (i + 1) * PIECE]
        key_grad = key_grad * scale
        for w, s in enumerate(slots):
            part = slice(w * BLOCK, (w + 1) * BLOCK)
            acc[pl.ds(s, BLOCK), :DIM] += key_grad[part]
            acc[pl.ds(s, BLOCK), DIM:] += value_grad[part]

    for ref, i in zip(parts, output_order(len(parts))):
        ref[...] = acc[starts[i] : starts[i + 1], :].astype(ref.dtype)


def attention(chain, place, pairing, live, docs, qg, halo):
    wide = 2 * DIM
    vmem = pl.BlockSpec(memory_space=pltpu.VMEM)
    smem = pl.BlockSpec(memory_space=pltpu.SMEM)
    starts = [0]
    for held in halo:
        starts.append(starts[-1] + held.shape[0])
    return pl.pallas_call(
        functools.partial(attention_kernel, chain, starts),
        out_shape=(
            jax.ShapeDtypeStruct((ROWS, QUERY_WIDE), jnp.bfloat16),
            jax.ShapeDtypeStruct((2, GROUP // 2, WINDOW * BLOCK, 2 * BLOCK), jnp.bfloat16),
            jax.ShapeDtypeStruct((2, DIM, WINDOW * BLOCK), jnp.bfloat16),
            jax.ShapeDtypeStruct((ROWS, wide), jnp.float32),
            *(
                jax.ShapeDtypeStruct(halo[i].shape, jnp.bfloat16)
                for i in output_order(len(halo))[1:]
            ),
        ),
        in_specs=[smem, smem] + [vmem] * (4 + len(halo)),
        out_specs=(vmem,) * (3 + len(halo)),
        scratch_shapes=[
            pltpu.VMEM((starts[-1], wide), jnp.bfloat16),
            pltpu.VMEM((starts[-1], wide), jnp.float32),
        ],
        compiler_params=pltpu.CompilerParams(vmem_limit_bytes=32 * 1024 * 1024),
        cost_estimate=pl.CostEstimate(
            flops=2 * 5 * 2 * WINDOW * GROUP * BLOCK * BLOCK * DIM,
            bytes_accessed=3 * 1024 * 1024,
            transcendentals=2 * WINDOW * GROUP * BLOCK * BLOCK,
        ),
        name="attention",
    )(place, pairing, live, *docs, qg, *halo)


def query_kernel(ds_ref, kt_ref, dq_ref):
    scale = 1.0 / math.sqrt(DIM)
    for b in range(2):
        for h in range(0, GROUP, 2):
            dq = dot(kt_ref[b], ds_ref[b, h // 2], 1, 0) * scale
            dq = dq.T.astype(jnp.bfloat16)
            for i in range(PARTS):
                head, lane = divmod(i, PARTS // 2)
                at = (h + head) * DIM
                dq_ref[rows_of(b, lane), at : at + DIM] = dq[i * PIECE : (i + 1) * PIECE]


def query_grad(dscores, keys_turned):
    vmem = pl.BlockSpec(memory_space=pltpu.VMEM)
    return pl.pallas_call(
        query_kernel,
        out_shape=jax.ShapeDtypeStruct((ROWS, QUERY_WIDE), jnp.bfloat16),
        in_specs=[vmem, vmem],
        out_specs=vmem,
        compiler_params=pltpu.CompilerParams(vmem_limit_bytes=32 * 1024 * 1024),
        name="query_grad",
    )(dscores, keys_turned)


def body(pairing, doc_start, block_live, query, key, value, grad_out):
    pairs = lax.axis_size("pair")
    chain = 2 * pairs
    blocks = 2 * chain
    pair = lax.axis_index("pair")
    side = lax.axis_index("side")
    half = lax.axis_index("half")

    axes = ("pair", "side", "half", "lane")
    lanes = lax.axis_size("lane")

    def device(place, head):
        in_half = int(place >= pairs)
        in_pair = chain - 1 - place if in_half else place
        here = next(p for p in range(PARTS) if head_of(p, in_half) == head)
        in_side, in_lane = divmod(here, lanes)
        return ((in_pair * 2 + in_side) * 2 + in_half) * lanes + in_lane

    def steps(by, targets):
        return [
            (device(s - by, head), device(s, head))
            for s in targets
            if 0 <= s - by < chain
            for head in range(PARTS)
        ]

    forth = [
        steps(1, range(chain)),
        steps(2, range(chain)),
        steps(3, range(pairs + 1, chain)),
        steps(-1, range(pairs, chain)),
    ]
    back = [[(b, a) for a, b in pairs_of] for pairs_of in forth]

    def move(x, pairs_of):
        return lax.ppermute(x, axes, pairs_of)

    def exchange(x):
        order = [[spot(p) for p in range(PARTS)]]
        return lax.all_to_all(
            x, ("side", "lane"), split_axis=0, concat_axis=0, axis_index_groups=order, tiled=True
        )

    place = jnp.stack([pair, side, half]).astype(jnp.int32)
    split = pack(query, grad_out, key, value)
    split, pairing, doc = lax.optimization_barrier((split, pairing, doc_start.reshape(1, ROWS)))
    doc_other = lax.ppermute(doc, "side", [(0, 1), (1, 0)])
    later = (half == 0) | (pairing[2 * pair + 1] < pairing[2 * pair])
    crossed = jnp.any(pairing[1 : chain - 1 : 2] == jnp.arange(2, chain, 2, dtype=jnp.int32))
    arrived = exchange(split).reshape(ROWS, WIDE)
    arrived, later, crossed, doc_other = lax.optimization_barrier(
        (arrived, later, crossed, doc_other)
    )

    def finish(with_crossed, place, later, pairing, block_live, doc, doc_other, arrived):
        own = arrived[:, QG_WIDE:WIDE].reshape(lanes, 2, PIECE, 2 * DIM)
        own = own.transpose(1, 0, 2, 3).reshape(ROWS, 2 * DIM)
        halo = [own, move(own, forth[0]), move(own, forth[1])]
        if with_crossed:
            halo.append(move(jnp.where(later, own[BLOCK:], own[:BLOCK]), forth[2]))
            halo.append(move(own[BLOCK:], forth[3]))
        att, dscores, keys_turned, *partials = attention(
            chain, place, pairing, block_live, (doc, doc_other), arrived, halo
        )
        moved = {}
        for i, part in zip(output_order(len(partials)), partials):
            moved[i] = move(part, back[i - 1]) if i else part
        dq = query_grad(dscores, keys_turned)
        total = gather(place, pairing, att, dq, [moved[i] for i in range(len(moved))])
        return unpack(exchange(total.reshape(PARTS, PIECE, -1)))

    return lax.cond(
        crossed,
        functools.partial(finish, True),
        functools.partial(finish, False),
        place,
        later,
        pairing,
        block_live,
        doc,
        doc_other,
        arrived,
    )


def solution(mesh):
    ctx, head = mesh.devices.shape
    fine = Mesh(mesh.devices.reshape(ctx // 2, 2, 2, head // 2), ("pair", "side", "half", "lane"))
    tokens = P(("pair", "side", "half", "lane"), None)
    return jax.shard_map(
        body,
        mesh=fine,
        in_specs=(P(), P(("pair", "side")), P(), tokens, tokens, tokens, tokens),
        out_specs=(tokens,) * 4,
        check_vma=False,
    )
```

```python
import functools
import math

import jax
import jax.numpy as jnp
from jax import lax
from jax.experimental import pallas as pl
from jax.experimental.pallas import tpu as pltpu
from jax.sharding import Mesh
from jax.sharding import PartitionSpec as P

DIM = 128
BLOCK = 128
REACH = 4
WINDOW = REACH + 1
GROUP = 4
PARTS = 8
ROWS = 2 * BLOCK
PIECE = ROWS // PARTS
NEGATIVE = -1e30
QUERY_WIDE = GROUP * DIM
QG_WIDE = 2 * QUERY_WIDE
WIDE = QG_WIDE + 2 * DIM


def dot(a, b, over_a, over_b):
    return lax.dot_general(
        a, b, (((over_a,), (over_b,)), ((), ())), preferred_element_type=jnp.float32
    )


def head_of(place, half):
    return (place + 2 * half) % PARTS


def spot(p):
    return p % 2 * (PARTS // 2) + p // 2


def rows_of(block, lane):
    first = (2 * lane + block) * PIECE
    return slice(first, first + PIECE)


def pieces(whole, split, at, wide):
    half = lax.axis_index("half")
    columns = [pl.multiple_of(head_of(spot(p), half) * wide, wide) for p in range(PARTS)]
    return [
        (whole.at[:, pl.ds(column, wide)], split.at[p, :, pl.ds(at, wide)])
        for p, column in enumerate(columns)
    ]


def copies_of(first, second, split, at, wide, sems, cut):
    pairs = pieces(first, split, at, wide) + pieces(second, split, at + wide, wide)
    return [
        pltpu.make_async_copy(*((rows, piece) if cut else (piece, rows)), sems.at[i])
        for i, (rows, piece) in enumerate(pairs)
    ]


def pack_kernel(q_ref, g_ref, k_ref, v_ref, out_ref, sems):
    copies = copies_of(q_ref, g_ref, out_ref, 0, QUERY_WIDE, sems, True)
    copies += copies_of(k_ref, v_ref, out_ref, QG_WIDE, DIM, sems.at[2 * PARTS :], True)
    for copy in copies:
        copy.start()
    for copy in copies:
        copy.wait()


def pack(query, grad_out, key, value):
    hbm = pl.BlockSpec(memory_space=pltpu.HBM)
    return pl.pallas_call(
        pack_kernel,
        out_shape=jax.ShapeDtypeStruct((PARTS, PIECE, WIDE), jnp.bfloat16),
        in_specs=[hbm] * 4,
        out_specs=pl.BlockSpec(memory_space=pltpu.VMEM),
        scratch_shapes=[pltpu.SemaphoreType.DMA((4 * PARTS,))],
        compiler_params=pltpu.CompilerParams(vmem_limit_bytes=(63 * 1024 + 256) * 1024),
        name="pack",
    )(query, grad_out, key, value)


def unpack_kernel(split_ref, att_ref, dq_ref, dk_ref, dv_ref, sems):
    copies = copies_of(att_ref, dq_ref, split_ref, 0, QUERY_WIDE, sems, False)
    copies += copies_of(dk_ref, dv_ref, split_ref, QG_WIDE, DIM, sems.at[2 * PARTS :], False)
    for copy in copies:
        copy.start()
    for copy in copies:
        copy.wait()


def unpack(split):
    hbm = pl.BlockSpec(memory_space=pltpu.HBM)
    wide = jax.ShapeDtypeStruct((PIECE, PARTS * QUERY_WIDE), jnp.bfloat16)
    narrow = jax.ShapeDtypeStruct((PIECE, PARTS * DIM), jnp.bfloat16)
    return pl.pallas_call(
        unpack_kernel,
        out_shape=(wide, wide, narrow, narrow),
        in_specs=[pl.BlockSpec(memory_space=pl.ANY)],
        out_specs=(hbm,) * 4,
        scratch_shapes=[pltpu.SemaphoreType.DMA((4 * PARTS,))],
        compiler_params=pltpu.CompilerParams(vmem_limit_bytes=16 * 1024 * 1024),
        name="unpack",
    )(split)


def gather_kernel(place_ref, pairing_ref, att_ref, dq_ref, own_ref, one_ref, two_ref, *refs):
    *extra, out_ref = refs
    out_ref[:, :QUERY_WIDE] = att_ref[...]
    out_ref[:, QUERY_WIDE:QG_WIDE] = dq_ref[...]
    total = own_ref[...] + one_ref[...].astype(jnp.float32) + two_ref[...].astype(jnp.float32)
    lower, upper = total[:BLOCK], total[BLOCK:]
    if extra:
        three_ref, back_ref = extra
        pair = place_ref[0]
        later = (place_ref[2] == 0) | (pairing_ref[2 * pair + 1] < pairing_ref[2 * pair])
        three = three_ref[...].astype(jnp.float32)
        lower = lower + jnp.where(later, 0.0, three)
        upper = upper + jnp.where(later, three, 0.0) + back_ref[...].astype(jnp.float32)
    for b, part in enumerate((lower, upper)):
        part = part.astype(jnp.bfloat16)
        for lane in range(PARTS // 2):
            out_ref[rows_of(b, lane), QG_WIDE:] = part[lane * PIECE : (lane + 1) * PIECE]


def gather(place, pairing, att, dq, parts):
    vmem = pl.BlockSpec(memory_space=pltpu.VMEM)
    smem = pl.BlockSpec(memory_space=pltpu.SMEM)
    return pl.pallas_call(
        gather_kernel,
        out_shape=jax.ShapeDtypeStruct((ROWS, QG_WIDE + 2 * DIM), jnp.bfloat16),
        in_specs=[smem, smem] + [vmem] * (2 + len(parts)),
        out_specs=vmem,
        compiler_params=pltpu.CompilerParams(vmem_limit_bytes=16 * 1024 * 1024),
        name="gather",
    )(place, pairing, att, dq, *parts)


def output_order(count):
    return [0, 2, 1, 3, 4][:count]


def attention_kernel(
    chain, starts, place_ref, pairing_ref, live_ref, doc_ref, doc_other_ref, qg_ref, *refs
):
    held = refs[: len(starts) - 1]
    od_ref, ds_ref, kt_ref, *parts, kv, acc = refs[len(starts) - 1 :]
    pair = place_ref[0]
    half = place_ref[2]
    blocks = 2 * chain
    ctx = chain
    scale = 1.0 / math.sqrt(DIM)
    my_place = jnp.where(half == 0, pair, chain - 1 - pair)

    for ref, begin, end in zip(held, starts, starts[1:]):
        kv[begin:end, :] = ref[...]
    acc[...] = jnp.zeros_like(acc)

    side = place_ref[1]
    mine = jnp.where(half == 0, doc_ref[:, :BLOCK], doc_ref[:, BLOCK:])
    other = jnp.where(half == 0, doc_other_ref[:, :BLOCK], doc_other_ref[:, BLOCK:])
    keys_down = lax.broadcasted_iota(jnp.int32, (BLOCK, BLOCK), 0)
    rows_along = lax.broadcasted_iota(jnp.int32, (BLOCK, BLOCK), 1)
    lanes = lax.broadcasted_iota(jnp.int32, (1, blocks), 1)

    for b in range(2):
        holder = 2 * pair + b
        block = jnp.where(half == 0, holder, blocks - 1 - pairing_ref[holder])
        begins = jnp.where(side == b, mine, other)
        live_row = live_ref[pl.ds(block, 1), :]
        slots = []
        bias = []
        for w in range(WINDOW):
            key_block = block - w
            mirrored = pairing_ref[jnp.clip(blocks - 1 - key_block, 0, ctx - 1)]
            held_by = jnp.where(key_block < ctx, key_block, mirrored)
            where_held = jnp.where(key_block < ctx, held_by // 2, chain - 1 - held_by // 2)
            away = my_place - where_held
            slot = jnp.where(away == 3, 6, jnp.where(away == -1, 7, 2 * away + held_by % 2))
            slot = jnp.where(key_block >= 0, jnp.clip(slot, 0, starts[-1] // BLOCK - 1), 0)
            slots.append(pl.multiple_of(slot * BLOCK, BLOCK))
            reach = begins - key_block * BLOCK
            if w == 0:
                seen = (keys_down >= reach) & (keys_down <= rows_along)
            else:
                listed = jnp.max(
                    jnp.where(lanes == key_block, live_row, 0), axis=1, keepdims=True
                )
                seen = keys_down >= jnp.where(listed == 1, reach, BLOCK)
            bias.append(jnp.where(seen, 0.0, NEGATIVE))
        bias = jnp.concatenate(bias, axis=0)
        bias = jnp.concatenate([bias, bias], axis=1)
        keys = jnp.concatenate([kv[pl.ds(s, BLOCK), :DIM] for s in slots], axis=0)
        values = jnp.concatenate([kv[pl.ds(s, BLOCK), DIM:] for s in slots], axis=0)
        keys_turned = keys.T
        values_turned = values.T
        kt_ref[b] = keys_turned
        lanes_of = [rows_of(b, lane) for lane in range(PARTS // 2)]
        key_grad = None
        value_grad = None
        for h in range(0, GROUP, 2):
            first, second = h * DIM, (h + 1) * DIM
            shift = GROUP * DIM
            columns = [slice(at, at + DIM) for at in (first, second)]
            g_columns = [slice(shift + at, shift + at + DIM) for at in (first, second)]
            q = jnp.concatenate([qg_ref[r, c] for c in columns for r in lanes_of], axis=0)
            g = jnp.concatenate([qg_ref[r, c] for c in g_columns for r in lanes_of], axis=0)
            scores = dot(keys, q, 1, 1) + bias
            peak = jnp.max(scores, axis=0, keepdims=True)
            p = jnp.exp2((scores - peak) * (scale * math.log2(math.e)))
            p = p * (1.0 / jnp.sum(p, axis=0, keepdims=True))
            weights = p.astype(jnp.bfloat16)
            out = dot(values_turned, weights, 1, 0)
            g_turned = g.astype(jnp.float32).T
            delta = jnp.sum(
                g_turned * out.astype(jnp.bfloat16).astype(jnp.float32), axis=0, keepdims=True
            )
            dweights = dot(values, g, 1, 1)
            dscores = (p * (dweights - delta)).astype(jnp.bfloat16)
            ds_ref[b, h // 2] = dscores
            key_new = dot(dscores, q, 1, 0)
            value_new = dot(weights, g, 1, 0)
            key_grad = key_new if key_grad is None else key_grad + key_new
            value_grad = value_new if value_grad is None else value_grad + value_new
            od_ref[b, h // 2] = out.astype(jnp.bfloat16)
        key_grad = key_grad * scale
        for w, s in enumerate(slots):
            part = slice(w * BLOCK, (w + 1) * BLOCK)
            acc[pl.ds(s, BLOCK), :DIM] += key_grad[part]
            acc[pl.ds(s, BLOCK), DIM:] += value_grad[part]

    for ref, i in zip(parts, output_order(len(parts))):
        ref[...] = acc[starts[i] : starts[i + 1], :].astype(ref.dtype)


def attention(chain, place, pairing, live, docs, qg, halo):
    wide = 2 * DIM
    vmem = pl.BlockSpec(memory_space=pltpu.VMEM)
    smem = pl.BlockSpec(memory_space=pltpu.SMEM)
    starts = [0]
    for held in halo:
        starts.append(starts[-1] + held.shape[0])
    return pl.pallas_call(
        functools.partial(attention_kernel, chain, starts),
        out_shape=(
            jax.ShapeDtypeStruct((2, GROUP // 2, DIM, 2 * BLOCK), jnp.bfloat16),
            jax.ShapeDtypeStruct((2, GROUP // 2, WINDOW * BLOCK, 2 * BLOCK), jnp.bfloat16),
            jax.ShapeDtypeStruct((2, DIM, WINDOW * BLOCK), jnp.bfloat16),
            jax.ShapeDtypeStruct((ROWS, wide), jnp.float32),
            *(
                jax.ShapeDtypeStruct(halo[i].shape, jnp.bfloat16)
                for i in output_order(len(halo))[1:]
            ),
        ),
        in_specs=[smem, smem] + [vmem] * (4 + len(halo)),
        out_specs=(vmem,) * (3 + len(halo)),
        scratch_shapes=[
            pltpu.VMEM((starts[-1], wide), jnp.bfloat16),
            pltpu.VMEM((starts[-1], wide), jnp.float32),
        ],
        compiler_params=pltpu.CompilerParams(vmem_limit_bytes=32 * 1024 * 1024),
        cost_estimate=pl.CostEstimate(
            flops=2 * 5 * 2 * WINDOW * GROUP * BLOCK * BLOCK * DIM,
            bytes_accessed=3 * 1024 * 1024,
            transcendentals=2 * WINDOW * GROUP * BLOCK * BLOCK,
        ),
        name="attention",
    )(place, pairing, live, *docs, qg, *halo)


def turn_kernel(out_ref, ds_ref, kt_ref, att_ref, dq_ref):
    scale = 1.0 / math.sqrt(DIM)
    for b in range(2):
        for h in range(0, GROUP, 2):
            out = out_ref[b, h // 2].astype(jnp.float32).T.astype(jnp.bfloat16)
            dq = dot(kt_ref[b], ds_ref[b, h // 2], 1, 0) * scale
            dq = dq.T.astype(jnp.bfloat16)
            for i in range(PARTS):
                head, lane = divmod(i, PARTS // 2)
                at = (h + head) * DIM
                att_ref[rows_of(b, lane), at : at + DIM] = out[i * PIECE : (i + 1) * PIECE]
                dq_ref[rows_of(b, lane), at : at + DIM] = dq[i * PIECE : (i + 1) * PIECE]


def turn(out, dscores, keys_turned):
    vmem = pl.BlockSpec(memory_space=pltpu.VMEM)
    shape = jax.ShapeDtypeStruct((ROWS, QUERY_WIDE), jnp.bfloat16)
    return pl.pallas_call(
        turn_kernel,
        out_shape=(shape, shape),
        in_specs=[vmem] * 3,
        out_specs=(vmem, vmem),
        compiler_params=pltpu.CompilerParams(vmem_limit_bytes=32 * 1024 * 1024),
        name="turn",
    )(out, dscores, keys_turned)


def body(pairing, doc_start, block_live, query, key, value, grad_out):
    pairs = lax.axis_size("pair")
    chain = 2 * pairs
    blocks = 2 * chain
    pair = lax.axis_index("pair")
    side = lax.axis_index("side")
    half = lax.axis_index("half")

    axes = ("pair", "side", "half", "lane")
    lanes = lax.axis_size("lane")

    def device(place, head):
        in_half = int(place >= pairs)
        in_pair = chain - 1 - place if in_half else place
        here = next(p for p in range(PARTS) if head_of(p, in_half) == head)
        in_side, in_lane = divmod(here, lanes)
        return ((in_pair * 2 + in_side) * 2 + in_half) * lanes + in_lane

    def steps(by, targets):
        return [
            (device(s - by, head), device(s, head))
            for s in targets
            if 0 <= s - by < chain
            for head in range(PARTS)
        ]

    forth = [
        steps(1, range(chain)),
        steps(2, range(chain)),
        steps(3, range(pairs + 1, chain)),
        steps(-1, range(pairs, chain)),
    ]
    back = [[(b, a) for a, b in pairs_of] for pairs_of in forth]

    def move(x, pairs_of):
        return lax.ppermute(x, axes, pairs_of)

    def exchange(x):
        order = [[spot(p) for p in range(PARTS)]]
        return lax.all_to_all(
            x, ("side", "lane"), split_axis=0, concat_axis=0, axis_index_groups=order, tiled=True
        )

    place = jnp.stack([pair, side, half]).astype(jnp.int32)
    split = pack(query, grad_out, key, value)
    split, pairing, doc = lax.optimization_barrier((split, pairing, doc_start.reshape(1, ROWS)))
    doc_other = lax.ppermute(doc, "side", [(0, 1), (1, 0)])
    later = (half == 0) | (pairing[2 * pair + 1] < pairing[2 * pair])
    crossed = jnp.any(pairing[1 : chain - 1 : 2] == jnp.arange(2, chain, 2, dtype=jnp.int32))
    arrived = exchange(split).reshape(ROWS, WIDE)
    arrived, later, crossed, doc_other = lax.optimization_barrier(
        (arrived, later, crossed, doc_other)
    )

    def finish(with_crossed, place, later, pairing, block_live, doc, doc_other, arrived):
        own = arrived[:, QG_WIDE:WIDE].reshape(lanes, 2, PIECE, 2 * DIM)
        own = own.transpose(1, 0, 2, 3).reshape(ROWS, 2 * DIM)
        halo = [own, move(own, forth[0]), move(own, forth[1])]
        if with_crossed:
            halo.append(move(jnp.where(later, own[BLOCK:], own[:BLOCK]), forth[2]))
            halo.append(move(own[BLOCK:], forth[3]))
        out, dscores, keys_turned, *partials = attention(
            chain, place, pairing, block_live, (doc, doc_other), arrived, halo
        )
        moved = {}
        for i, part in zip(output_order(len(partials)), partials):
            moved[i] = move(part, back[i - 1]) if i else part
        att, dq = turn(out, dscores, keys_turned)
        total = gather(place, pairing, att, dq, [moved[i] for i in range(len(moved))])
        return unpack(exchange(total.reshape(PARTS, PIECE, -1)))

    return lax.cond(
        crossed,
        functools.partial(finish, True),
        functools.partial(finish, False),
        place,
        later,
        pairing,
        block_live,
        doc,
        doc_other,
        arrived,
    )


def solution(mesh):
    ctx, head = mesh.devices.shape
    fine = Mesh(mesh.devices.reshape(ctx // 2, 2, 2, head // 2), ("pair", "side", "half", "lane"))
    tokens = P(("pair", "side", "half", "lane"), None)
    return jax.shard_map(
        body,
        mesh=fine,
        in_specs=(P(), P(("pair", "side")), P(), tokens, tokens, tokens, tokens),
        out_specs=(tokens,) * 4,
        check_vma=False,
    )
```
